32 devices in a mesh: dp: 4 (over z), mp: 8 (over y, x, core).
Axes of the slice: x: 2, y: 2, z: 4, core: 2. Of those that a mesh axis runs over, the one named last changes fastest.
Arguments:
- tokens: bfloat16 [1024, 8192], P('dp', 'mp'), may hold values from -6 to 6
- router_weight: bfloat16 [8192, 64], P('mp'), may hold values from -0.0625 to 0.0625
- gate_cotangent: float32 [1024, 2], P('dp'), may hold values from -6 to 6
- expert_index: int32 [1024, 2], P('dp'), may hold values from 0 to 63, as said below
- slot_index: int32 [1024, 2], P('dp'), may hold values from -1 to 9, as said below
Outputs:
- gates: float32 [1024, 2], P(('dp', 'mp'))
- router_grad: float32 [8192, 64], P('mp')
- dispatched: bfloat16 [4, 64, 10, 8192], P('dp', 'mp')
The draws below stay inside these ranges and needn't reach their ends.
Inputs may be any that keep to these rules, and one draw needn't show every extreme that they name: `expert_index`: the two picks of a token are different experts. `slot_index`: for each group, the picks are ranked per expert with all first picks in token order before all second picks in token order; a pick's slot is its rank if that is below 10, else -1. In every group some expert is picked more than 10 times, so its 10 slots are all filled.
All inputs are finite; a program needn't handle non-finite values.
Results may differ from the reference program's by a relative error of at most 0.0029.
Values may be sent and summed in bfloat16 or wider, within the bound.
A program may use at most 64 MiB of HBM per device.

```python
import jax
import jax.numpy as jnp
from jax import lax

D = 8192
E = 64
GROUP_TOK = 256
GROUPS = 4
TOKENS = 1024
CAP = 10


def routing_tables(key):
    base_key = jax.random.fold_in(key, 7)
    kbase, kheavy, kdraw, ksecond = jax.random.split(base_key, 4)
    levels = jnp.arange(E, dtype=jnp.int32)
    base = jax.random.randint(kbase, (GROUPS, E), 1, 5)
    heavy = jax.random.randint(kheavy, (), 0, E)
    rising = 12 + 24 * jnp.arange(GROUPS, dtype=jnp.int32) // max(GROUPS - 1, 1)
    weights = base + (levels[None, :] == heavy).astype(jnp.int32) * rising[:, None]
    bounds = jnp.cumsum(weights, axis=1)
    totals = bounds[:, -1]
    raw = jax.random.randint(kdraw, (GROUPS, GROUP_TOK), 0, 1 << 20)
    drawn = raw % totals[:, None]
    first = jnp.sum((drawn[:, :, None] >= bounds[:, None, :]).astype(jnp.int32), axis=2)
    second = (first + 1 + jax.random.randint(ksecond, (GROUPS, GROUP_TOK), 0, E - 1)) % E
    ordered = jnp.concatenate([first, second], axis=1)
    onehot = (ordered[:, :, None] == levels[None, None, :]).astype(jnp.int32)
    ranked = jnp.cumsum(onehot, axis=1) - onehot
    place = jnp.sum(ranked * onehot, axis=2)
    place = jnp.where(place < CAP, place, -1)
    picks = jnp.stack([first, second], axis=2).reshape(TOKENS, 2)
    slots = jnp.stack([place[:, :GROUP_TOK], place[:, GROUP_TOK:]], axis=2).reshape(TOKENS, 2)
    return (picks.astype(jnp.int32), slots.astype(jnp.int32))


def draw_expert_index(key, part):
    return routing_tables(key)[0]


def draw_slot_index(key, part):
    return routing_tables(key)[1]


def block_scale(key, extent, cuts, least, largest):
    factor_of, own = 1.0, jax.random.fold_in(key, 6)
    for axis_at, blocks in cuts:
        heights = jnp.exp(jax.random.uniform(jax.random.fold_in(own, axis_at), (blocks,), jnp.float32, least / len(cuts), largest / len(cuts)))
        factor_of = factor_of * jnp.repeat(heights, extent[axis_at] // blocks).reshape([-1 if axis == axis_at else 1 for axis in range(len(extent))])
    return factor_of


def noise(rng, dims, width, bound, shards=(), kind=jnp.bfloat16):
    entries = width * jax.random.normal(rng, dims, jnp.float32)
    if shards:
        entries = entries * block_scale(rng, dims, shards, -0.22, 0.18)
    return jnp.clip(entries, -bound, bound).astype(kind)


def setup_inputs(seed: int = 0) -> dict:
    streams_of = jax.random.split(jax.random.key(seed), 6)
    tokens = noise(streams_of[0], (TOKENS, D), 1.0, 6.0, ((0, 4), (1, 8)))
    router_weight = noise(streams_of[1], (D, E), D ** -0.5, 0.0625, ((0, 8),))
    gate_cotangent = noise(streams_of[2], (TOKENS, 2), 1.0, 6.0, ((0, 4),), jnp.float32)
    expert_index = draw_expert_index(jax.random.fold_in(streams_of[5], 71), 0)
    slot_index = draw_slot_index(jax.random.fold_in(streams_of[5], 71), 0)
    return dict(tokens=tokens, router_weight=router_weight, gate_cotangent=gate_cotangent, expert_index=expert_index, slot_index=slot_index)


balance_weight = 0.5
zloss_weight = 0.02

def route_grad(logits, cotangent, picks, load):
    levels = jnp.arange(logits.shape[1], dtype=jnp.int32)
    expo = jnp.exp(logits)
    total = lax.optimization_barrier(jnp.sum(expo, axis=1, keepdims=True))
    probs = expo / total
    lse = jnp.log(total)
    first = (picks[:, 0:1] == levels[None, :]).astype(jnp.float32)
    second = (picks[:, 1:2] == levels[None, :]).astype(jnp.float32)
    pfirst = lax.optimization_barrier(jnp.sum(probs * first, axis=1, keepdims=True))
    psecond = lax.optimization_barrier(jnp.sum(probs * second, axis=1, keepdims=True))
    denom = pfirst + psecond
    gfirst = pfirst / denom
    gsecond = psecond / denom
    cfirst = cotangent[:, 0:1]
    csecond = cotangent[:, 1:2]
    mixed = cfirst * gfirst + csecond * gsecond
    upward = first * (cfirst - mixed) / denom + second * (csecond - mixed) / denom + balance_weight * load[None, :]
    inner = lax.optimization_barrier(jnp.sum(probs * upward, axis=1, keepdims=True))
    grad = probs * (upward - inner) + 2.0 * zloss_weight * lse * probs
    gates = jnp.concatenate([gfirst, gsecond], axis=1)
    return (gates, grad.astype(jnp.bfloat16))

def reference(tokens, router_weight, gate_cotangent, expert_index, slot_index):
    logits = jnp.dot(tokens, router_weight, preferred_element_type=jnp.float32)
    levels = jnp.arange(E, dtype=jnp.int32)
    counts = lax.optimization_barrier(jnp.sum((expert_index[:, :, None] == levels[None, None, :]).astype(jnp.float32), axis=(0, 1)))
    load = counts * E / (2.0 * TOKENS)
    gates, grad = route_grad(logits, gate_cotangent, expert_index, load)
    router_grad = jnp.dot(tokens.T, grad, preferred_element_type=jnp.float32)
    cell = jnp.where(slot_index >= 0, expert_index * CAP + slot_index, E * CAP).astype(jnp.int32)
    group = (jnp.arange(TOKENS, dtype=jnp.int32) // GROUP_TOK).astype(jnp.int32)
    buffer = jnp.zeros((GROUPS, E * CAP + 1, D), jnp.bfloat16)
    buffer = buffer.at[group, cell[:, 0]].set(tokens)
    buffer = buffer.at[group, cell[:, 1]].set(tokens)
    dispatched = buffer[:, :E * CAP].reshape(GROUPS, E, CAP, D)
    return (gates, router_grad, dispatched)
```

```python
import functools

import jax
import jax.numpy as jnp
from jax import lax
from jax.experimental import pallas as pl
from jax.experimental.pallas import tpu as pltpu
from jax.sharding import PartitionSpec as P

balance_weight = 0.5
zloss_weight = 0.02
MESH = pl.DeviceIdType.MESH


def route_grad(logits, cotangent, picks, load):
    levels = lax.broadcasted_iota(jnp.int32, logits.shape, 1)
    expo = jnp.exp(logits)
    total = jnp.sum(expo, axis=1, keepdims=True)
    probs = expo / total
    lse = jnp.log(total)
    first = (picks[:, 0:1] == levels).astype(jnp.float32)
    second = (picks[:, 1:2] == levels).astype(jnp.float32)
    pfirst = jnp.sum(probs * first, axis=1, keepdims=True)
    psecond = jnp.sum(probs * second, axis=1, keepdims=True)
    denom = pfirst + psecond
    gfirst = pfirst / denom
    gsecond = psecond / denom
    cfirst = cotangent[:, 0:1]
    csecond = cotangent[:, 1:2]
    mixed = cfirst * gfirst + csecond * gsecond
    upward = (
        first * (cfirst - mixed) / denom
        + second * (csecond - mixed) / denom
        + balance_weight * load
    )
    inner = jnp.sum(probs * upward, axis=1, keepdims=True)
    grad = probs * (upward - inner) + 2.0 * zloss_weight * lse * probs
    return gfirst, gsecond, grad.astype(jnp.bfloat16)


def flip(index, mask, size):
    out = index
    bit = 1
    while bit < size:
        if mask & bit:
            out = out + bit * (1 - 2 * ((index // bit) % 2))
        bit *= 2
    return out


def exchange(
    n, d, capacity,
    tok_ref, w_ref, cot_ref, pick_ref, slot_ref,
    gates_ref, wgrad_ref, slots_ref,
    lg_send, lg_recv, cnt_send, cnt_recv, own_grad, grads, rows_send, part_send, part_recv, own_wgrad,
    cnt_ss, cnt_rs, lg_ss, lg_rs, gr_ss, gr_rs, a2a_ss, a2a_rs, rs_ss, rs_rs, ag_ss, ag_rs,
):
    me = lax.axis_index("mp")
    my_dp = lax.axis_index("dp")
    rows, feats = tok_ref.shape
    experts = w_ref.shape[1]
    own = rows // n
    half = own // 2
    width = rows_send.shape[1]
    eper = experts // d
    mp_order = list(range(n - 1, 0, -1))
    dp_order = list(range(d - 1, 0, -1))

    def to_mp(k):
        return {"dp": my_dp, "mp": flip(me, k, n)}

    def to_dp(k):
        return {"dp": flip(my_dp, k, d), "mp": me}

    barrier = pltpu.get_barrier_semaphore()
    for k in mp_order:
        pl.semaphore_signal(barrier, inc=1, device_id=to_mp(k), device_id_type=MESH)
    for k in dp_order:
        pl.semaphore_signal(barrier, inc=1, device_id=to_dp(k), device_id_type=MESH)

    partial_value = jnp.dot(tok_ref[...], w_ref[...], preferred_element_type=jnp.float32)
    for p in range(n):
        lo = partial_value[p * own : p * own + half]
        hi = partial_value[p * own + half : (p + 1) * own]
        lg_send[p] = jnp.concatenate([lo, hi], axis=1)
    picks = pick_ref[...]
    levels = lax.broadcasted_iota(jnp.int32, (rows, experts), 1)
    hot = (picks[:, 0:1] == levels).astype(jnp.float32) + (picks[:, 1:2] == levels).astype(jnp.float32)
    local = jnp.sum(hot, axis=0, keepdims=True)
    cnt_send[...] = jnp.broadcast_to(jnp.concatenate([local, local], axis=1), cnt_send.shape)

    pl.semaphore_wait(barrier, n - 1 + d - 1)

    lg = {}
    for k in mp_order:
        lg[k] = pltpu.make_async_remote_copy(
            src_ref=lg_send.at[flip(me, k, n)], dst_ref=lg_recv.at[k],
            send_sem=lg_ss.at[k], recv_sem=lg_rs.at[k], device_id=to_mp(k), device_id_type=MESH)
        lg[k].start()
    cnt = {}
    for k in dp_order:
        cnt[k] = pltpu.make_async_remote_copy(
            src_ref=cnt_send, dst_ref=cnt_recv.at[k],
            send_sem=cnt_ss.at[k], recv_sem=cnt_rs.at[k], device_id=to_dp(k), device_id_type=MESH)
        cnt[k].start()

    slots = slot_ref[...]
    cell = jnp.where(slots >= 0, picks * capacity + slots, -1)
    cell_a = jnp.transpose(jnp.broadcast_to(cell[:, 0:1], (rows, 128)))[:width]
    cell_b = jnp.transpose(jnp.broadcast_to(cell[:, 1:2], (rows, 128)))[:width]
    place = lax.broadcasted_iota(jnp.int32, (width, rows), 0)

    def fill(owner):
        target = place + owner * width
        onehot = ((cell_a == target) | (cell_b == target)).astype(jnp.float32).astype(jnp.bfloat16)
        return jnp.dot(onehot, tok_ref[...], preferred_element_type=jnp.float32).astype(jnp.bfloat16)

    columns = pl.ds(pl.multiple_of(me * feats, feats), feats)
    a2a = {}
    for k in mp_order:
        rows_send[k] = fill(flip(me, k, n))
        a2a[k] = pltpu.make_async_remote_copy(
            src_ref=rows_send.at[k], dst_ref=slots_ref.at[:, columns],
            send_sem=a2a_ss.at[k], recv_sem=a2a_rs.at[k], device_id=to_mp(k), device_id_type=MESH)
        a2a[k].start()
    slots_ref[:, columns] = fill(me)

    for k in dp_order:
        cnt[k].wait()
    counts = cnt_send[...]
    for k in dp_order:
        counts = counts + cnt_recv[k]
    load = counts[0:1, :experts] * experts / (2.0 * rows * d)
    for k in mp_order:
        lg[k].wait()
    packed = lg_send[me]
    for k in mp_order:
        packed = packed + lg_recv[k]
    logits = jnp.concatenate([packed[:, :experts], packed[:, experts:]], axis=0)
    mine = pl.ds(pl.multiple_of(me * own, own), own)
    gfirst, gsecond, grad = route_grad(logits, cot_ref[mine, :], pick_ref[mine, :], load)
    own_grad[...] = grad
    grads[mine, :] = grad
    gr = {}
    for k in mp_order:
        gr[k] = pltpu.make_async_remote_copy(
            src_ref=own_grad, dst_ref=grads.at[mine, :],
            send_sem=gr_ss.at[k], recv_sem=gr_rs.at[k], device_id=to_mp(k), device_id_type=MESH)
        gr[k].start()
    gates_ref[...] = jnp.concatenate([gfirst, gsecond], axis=1)
    for k in mp_order:
        gr[k].wait()

    part = lax.dot_general(
        grads[...], tok_ref[...], (((0,), (0,)), ((), ())), preferred_element_type=jnp.float32)
    for j in range(d):
        part_send[j] = part[j * eper : (j + 1) * eper]
    rs = {}
    for k in dp_order:
        rs[k] = pltpu.make_async_remote_copy(
            src_ref=part_send.at[flip(my_dp, k, d)], dst_ref=part_recv.at[k],
            send_sem=rs_ss.at[k], recv_sem=rs_rs.at[k], device_id=to_dp(k), device_id_type=MESH)
        rs[k].start()
    for k in dp_order:
        rs[k].wait()
    total = part_send[my_dp]
    for k in dp_order:
        total = total + part_recv[k]
    total = total.astype(jnp.bfloat16)
    own_wgrad[...] = total
    wgrad_ref[my_dp] = total
    ag = {}
    for k in dp_order:
        ag[k] = pltpu.make_async_remote_copy(
            src_ref=own_wgrad, dst_ref=wgrad_ref.at[my_dp],
            send_sem=ag_ss.at[k], recv_sem=ag_rs.at[k], device_id=to_dp(k), device_id_type=MESH)
        ag[k].start()
    for k in dp_order:
        ag[k].wait()
    for k in mp_order:
        a2a[k].wait()


def arrange(d, eper, capacity, gates_ref, wgrad_ref, slots_ref, gates_out, wgrad_out, slots_out):
    @pl.when(pl.program_id(0) == 0)
    def _():
        gates_out[...] = gates_ref[...]
        whole = jnp.concatenate([wgrad_ref[j].astype(jnp.float32) for j in range(d)], axis=0)
        wgrad_out[...] = jnp.transpose(whole)

    for e in range(slots_out.shape[1]):
        slots_out[0, e] = slots_ref[e * capacity : (e + 1) * capacity, :]


def on_device(n, d, tokens, router_weight, gate_cotangent, expert_index, slot_index):
    rows, feats = tokens.shape
    experts = router_weight.shape[1]
    own = rows // n
    capacity = 5 * rows // (2 * experts)
    owned = experts // n
    width = owned * capacity
    eper = experts // d
    bf16, f32 = jnp.bfloat16, jnp.float32
    dma = pltpu.SemaphoreType.DMA
    vmem = pl.BlockSpec(memory_space=pltpu.VMEM)
    gates, wgrad, slotted = pl.pallas_call(
        functools.partial(exchange, n, d, capacity),
        out_shape=(
            jax.ShapeDtypeStruct((own, 2), f32),
            jax.ShapeDtypeStruct((d, eper, feats), bf16),
            jax.ShapeDtypeStruct((width, n * feats), bf16),
        ),
        in_specs=[vmem] * 5,
        out_specs=(vmem, vmem, vmem),
        scratch_shapes=[
            pltpu.VMEM((n, own // 2, 2 * experts), f32),
            pltpu.VMEM((n, own // 2, 2 * experts), f32),
            pltpu.VMEM((8, 2 * experts), f32),
            pltpu.VMEM((d, 8, 2 * experts), f32),
            pltpu.VMEM((own, experts), bf16),
            pltpu.VMEM((rows, experts), bf16),
            pltpu.VMEM((n, width, feats), bf16),
            pltpu.VMEM((d, eper, feats), f32),
            pltpu.VMEM((d, eper, feats), f32),
            pltpu.VMEM((eper, feats), bf16),
            dma((d,)), dma((d,)), dma((n,)), dma((n,)), dma((n,)), dma((n,)),
            dma((n,)), dma((n,)), dma((d,)), dma((d,)), dma((d,)), dma((d,)),
        ],
        compiler_params=pltpu.CompilerParams(
            collective_id=0, has_side_effects=True, vmem_limit_bytes=24 * 1024 * 1024
        ),
        name="exchange",
    )(tokens, router_weight, gate_cotangent, expert_index, slot_index)
    steps = 4
    block = n * feats // steps
    gates, router_grad, dispatched = pl.pallas_call(
        functools.partial(arrange, d, eper, capacity),
        grid=(steps,),
        out_shape=(
            jax.ShapeDtypeStruct((own, 2), f32),
            jax.ShapeDtypeStruct((feats, experts), f32),
            jax.ShapeDtypeStruct((1, owned, capacity, n * feats), bf16),
        ),
        in_specs=[
            pl.BlockSpec((own, 2), lambda i: (0, 0)),
            pl.BlockSpec((d, eper, feats), lambda i: (0, 0, 0)),
            pl.BlockSpec((width, block), lambda i: (0, i)),
        ],
        out_specs=(
            pl.BlockSpec((own, 2), lambda i: (0, 0)),
            pl.BlockSpec((feats, experts), lambda i: (0, 0)),
            pl.BlockSpec((1, owned, capacity, block), lambda i: (0, 0, 0, i)),
        ),
        compiler_params=pltpu.CompilerParams(vmem_limit_bytes=16 * 1024 * 1024),
        name="arrange",
    )(gates, wgrad, slotted)
    return gates, router_grad, dispatched


def solution(mesh):
    n, d = mesh.shape["mp"], mesh.shape["dp"]
    in_specs = (P("dp", "mp"), P("mp", None), P("dp", None), P("dp", None), P("dp", None))
    out_specs = (P(("dp", "mp"), None), P("mp", None), P("dp", "mp", None, None))
    return jax.shard_map(
        functools.partial(on_device, n, d),
        mesh=mesh, in_specs=in_specs, out_specs=out_specs, check_vma=False,
    )
```

```python
import functools

import jax
import jax.numpy as jnp
from jax import lax
from jax.experimental import pallas as pl
from jax.experimental.pallas import tpu as pltpu
from jax.sharding import PartitionSpec as P

balance_weight = 0.5
zloss_weight = 0.02
MESH = pl.DeviceIdType.MESH


def route_grad(logits, cotangent, picks, load):
    levels = lax.broadcasted_iota(jnp.int32, logits.shape, 1).astype(jnp.float32)
    expo = jnp.exp(logits)
    total = jnp.sum(expo, axis=1, keepdims=True)
    probs = expo / total
    lse = jnp.log(total)
    first = (picks[:, 0:1] == levels).astype(jnp.float32)
    second = (picks[:, 1:2] == levels).astype(jnp.float32)
    pfirst = jnp.sum(probs * first, axis=1, keepdims=True)
    psecond = jnp.sum(probs * second, axis=1, keepdims=True)
    denom = pfirst + psecond
    gfirst = pfirst / denom
    gsecond = psecond / denom
    cfirst = cotangent[:, 0:1]
    csecond = cotangent[:, 1:2]
    mixed = cfirst * gfirst + csecond * gsecond
    upward = (
        first * (cfirst - mixed) / denom
        + second * (csecond - mixed) / denom
        + balance_weight * load
    )
    inner = jnp.sum(probs * upward, axis=1, keepdims=True)
    grad = probs * (upward - inner) + 2.0 * zloss_weight * lse * probs
    return gfirst, gsecond, grad.astype(jnp.bfloat16)


def flip(index, mask, size):
    out = index
    bit = 1
    while bit < size:
        if mask & bit:
            out = out + bit * (1 - 2 * ((index // bit) % 2))
        bit *= 2
    return out


def exchange(
    n, d, capacity, owned,
    tok_hbm, w_hbm, cot_ref, pick_ref, slot_ref,
    gates_ref, wgrad_ref, slots_ref,
    tok_ref, w_ref, aux_rows, aux,
    lg_send, lg_recv, cnt_send, cnt_recv, own_grad, grads, rows_send, part_send, part_recv, own_wgrad, wgrads,
    in_sems, cnt_ss, cnt_rs, lg_ss, lg_rs, gr_ss, gr_rs, a2a_ss, a2a_rs, rs_ss, rs_rs, ag_ss, ag_rs,
):
    me = lax.axis_index("mp")
    my_dp = lax.axis_index("dp")
    rows, feats = tok_ref.shape
    experts = w_ref.shape[0]
    own = rows // n
    half = own // 2
    width = owned * capacity
    eper = experts // d
    f32, bf16 = jnp.float32, jnp.bfloat16
    mp_order = list(range(n - 1, 0, -1))
    dp_order = list(range(d - 1, 0, -1))
    early = [k for k in (1, 2, 4) if k < n]
    late = [k for k in mp_order if k not in early]

    def to_mp(k):
        return {"dp": my_dp, "mp": flip(me, k, n)}

    def to_dp(k):
        return {"dp": flip(my_dp, k, d), "mp": me}

    tok_in = pltpu.make_async_copy(tok_hbm, tok_ref, in_sems.at[0])
    w_in = pltpu.make_async_copy(w_hbm, w_ref, in_sems.at[1])
    tok_in.start()
    w_in.start()
    barrier = pltpu.get_barrier_semaphore()
    for k in mp_order:
        pl.semaphore_signal(barrier, inc=1, device_id=to_mp(k), device_id_type=MESH)
    for k in dp_order:
        pl.semaphore_signal(barrier, inc=1, device_id=to_dp(k), device_id_type=MESH)

    picks = pick_ref[...]
    aux_rows[...] = jnp.zeros_like(aux_rows)
    aux_rows[0:2] = picks.astype(f32)
    aux_rows[2:4] = cot_ref[...]
    aux[...] = jnp.transpose(aux_rows[...])
    levels = lax.broadcasted_iota(jnp.int32, (experts, rows), 0)
    hot = (picks[0:1] == levels).astype(f32) + (picks[1:2] == levels).astype(f32)
    local = lax.dot_general(
        jnp.ones((8, rows), bf16), hot.astype(bf16), (((1,), (1,)), ((), ())), preferred_element_type=f32)
    cnt_send[...] = jnp.concatenate([local, local], axis=1)
    slots = slot_ref[...]
    owner_of = lax.div(picks, jnp.int32(owned))
    cell = jnp.where(slots >= 0, owner_of * width + slots * owned + picks - owner_of * owned, -1)
    place = lax.broadcasted_iota(jnp.int32, (width, rows), 0)

    w_in.wait()
    tok_in.wait()
    partial_value = lax.dot_general(
        tok_ref[...], w_ref[...], (((1,), (1,)), ((), ())), preferred_element_type=f32)
    for p in range(n):
        lo = partial_value[p * own : p * own + half]
        hi = partial_value[p * own + half : (p + 1) * own]
        lg_send[p] = jnp.concatenate([lo, hi], axis=1)

    pl.semaphore_wait(barrier, n - 1 + d - 1)

    lg = {}
    for k in mp_order:
        lg[k] = pltpu.make_async_remote_copy(
            src_ref=lg_send.at[flip(me, k, n)], dst_ref=lg_recv.at[k],
            send_sem=lg_ss.at[k], recv_sem=lg_rs.at[k], device_id=to_mp(k), device_id_type=MESH)
        lg[k].start()
    cnt = {}
    for k in dp_order:
        cnt[k] = pltpu.make_async_remote_copy(
            src_ref=cnt_send, dst_ref=cnt_recv.at[k],
            send_sem=cnt_ss.at[k], recv_sem=cnt_rs.at[k], device_id=to_dp(k), device_id_type=MESH)
        cnt[k].start()

    def fill(owner):
        target = place + owner * width
        onehot = ((cell[0:1] == target) | (cell[1:2] == target)).astype(f32).astype(bf16)
        return jnp.dot(onehot, tok_ref[...], preferred_element_type=f32).astype(bf16)

    columns = pl.ds(pl.multiple_of(me * feats, feats), feats)
    a2a = {}

    def push(k):
        a2a[k] = pltpu.make_async_remote_copy(
            src_ref=rows_send.at[k], dst_ref=slots_ref.at[:, columns],
            send_sem=a2a_ss.at[k], recv_sem=a2a_rs.at[k], device_id=to_mp(k), device_id_type=MESH)
        a2a[k].start()

    for k in early:
        rows_send[k] = fill(flip(me, k, n))
        push(k)
    for k in late:
        rows_send[k] = fill(flip(me, k, n))

    for k in dp_order:
        cnt[k].wait()
    counts = cnt_send[...]
    for k in dp_order:
        counts = counts + cnt_recv[k]
    load = counts[0:1, :experts] * experts / (2.0 * rows * d)
    for k in mp_order:
        lg[k].wait()
    packed = lg_send[me]
    for k in mp_order:
        packed = packed + lg_recv[k]
    logits = jnp.concatenate([packed[:, :experts], packed[:, experts:]], axis=0)
    mine = pl.ds(pl.multiple_of(me * own, own), own)
    side = aux[mine, :]
    gfirst, gsecond, grad = route_grad(logits, side[:, 2:4], side[:, 0:2], load)
    own_grad[...] = grad
    grads[mine, :] = grad
    gr = {}
    for k in mp_order:
        gr[k] = pltpu.make_async_remote_copy(
            src_ref=own_grad, dst_ref=grads.at[mine, :],
            send_sem=gr_ss.at[k], recv_sem=gr_rs.at[k], device_id=to_mp(k), device_id_type=MESH)
        gr[k].start()
    for k in late:
        push(k)
    slots_ref[:, columns] = fill(me)
    gates_ref[0:1] = jnp.transpose(jnp.broadcast_to(gfirst, (own, 128)))[0:1]
    gates_ref[1:2] = jnp.transpose(jnp.broadcast_to(gsecond, (own, 128)))[0:1]
    for k in mp_order:
        gr[k].wait()

    part = lax.dot_general(
        grads[...], tok_ref[...], (((0,), (0,)), ((), ())), preferred_element_type=f32)
    for j in range(d):
        part_send[j] = part[j * eper : (j + 1) * eper]
    rs = {}
    for k in dp_order:
        rs[k] = pltpu.make_async_remote_copy(
            src_ref=part_send.at[flip(my_dp, k, d)], dst_ref=part_recv.at[k],
            send_sem=rs_ss.at[k], recv_sem=rs_rs.at[k], device_id=to_dp(k), device_id_type=MESH)
        rs[k].start()
    for k in dp_order:
        rs[k].wait()
    total = part_send[my_dp]
    for k in dp_order:
        total = total + part_recv[k]
    total = total.astype(bf16)
    own_wgrad[...] = total
    wgrads[my_dp] = total
    ag = {}
    for k in dp_order:
        ag[k] = pltpu.make_async_remote_copy(
            src_ref=own_wgrad, dst_ref=wgrads.at[my_dp],
            send_sem=ag_ss.at[k], recv_sem=ag_rs.at[k], device_id=to_dp(k), device_id_type=MESH)
        ag[k].start()
    for k in dp_order:
        ag[k].wait()
    for j in range(d):
        wgrad_ref[j * eper : (j + 1) * eper] = wgrads[j].astype(f32)
    for k in mp_order:
        a2a[k].wait()


def on_device(n, d, tokens, router_weight, gate_cotangent, expert_index, slot_index):
    rows, feats = tokens.shape
    experts = router_weight.shape[1]
    own = rows // n
    capacity = 5 * rows // (2 * experts)
    owned = experts // n
    width = owned * capacity
    eper = experts // d
    bf16, f32 = jnp.bfloat16, jnp.float32
    dma = pltpu.SemaphoreType.DMA
    vmem = pl.BlockSpec(memory_space=pltpu.VMEM)
    hbm = pl.BlockSpec(memory_space=pltpu.HBM)
    gates, wgrad, slotted = pl.pallas_call(
        functools.partial(exchange, n, d, capacity, owned),
        out_shape=(
            jax.ShapeDtypeStruct((2, own), f32),
            jax.ShapeDtypeStruct((experts, feats), f32),
            jax.ShapeDtypeStruct((width, n * feats), bf16),
        ),
        in_specs=[hbm, hbm, vmem, vmem, vmem],
        out_specs=(vmem, vmem, vmem),
        scratch_shapes=[
            pltpu.VMEM((rows, feats), bf16),
            pltpu.VMEM((experts, feats), bf16),
            pltpu.VMEM((8, rows), f32),
            pltpu.VMEM((rows, 8), f32),
            pltpu.VMEM((n, own // 2, 2 * experts), f32),
            pltpu.VMEM((n, own // 2, 2 * experts), f32),
            pltpu.VMEM((8, 2 * experts), f32),
            pltpu.VMEM((d, 8, 2 * experts), f32),
            pltpu.VMEM((own, experts), bf16),
            pltpu.VMEM((rows, experts), bf16),
            pltpu.VMEM((n, width, feats), bf16),
            pltpu.VMEM((d, eper, feats), f32),
            pltpu.VMEM((d, eper, feats), f32),
            pltpu.VMEM((eper, feats), bf16),
            pltpu.VMEM((d, eper, feats), bf16),
            dma((2,)),
            dma((d,)), dma((d,)), dma((n,)), dma((n,)), dma((n,)), dma((n,)),
            dma((n,)), dma((n,)), dma((d,)), dma((d,)), dma((d,)), dma((d,)),
        ],
        compiler_params=pltpu.CompilerParams(
            collective_id=0, has_side_effects=True, vmem_limit_bytes=24 * 1024 * 1024
        ),
        name="exchange",
    )(tokens, router_weight.T, gate_cotangent.T, expert_index.T, slot_index.T)
    dispatched = slotted.reshape(1, capacity, owned, n * feats).transpose(0, 2, 1, 3)
    return gates.T, wgrad.T, dispatched


def solution(mesh):
    n, d = mesh.shape["mp"], mesh.shape["dp"]
    in_specs = (P("dp", "mp"), P("mp", None), P("dp", None), P("dp", None), P("dp", None))
    out_specs = (P(("dp", "mp"), None), P("mp", None), P("dp", "mp", None, None))
    return jax.shard_map(
        functools.partial(on_device, n, d),
        mesh=mesh, in_specs=in_specs, out_specs=out_specs, check_vma=False,
    )
```

```python
import functools

import jax
import jax.numpy as jnp
from jax import lax
from jax.experimental import pallas as pl
from jax.experimental.pallas import tpu as pltpu
from jax.sharding import PartitionSpec as P

balance_weight = 0.5
zloss_weight = 0.02
MESH = pl.DeviceIdType.MESH


def route_grad(logits, cotangent, picks, load):
    levels = lax.broadcasted_iota(jnp.int32, logits.shape, 1).astype(jnp.float32)
    expo = jnp.exp(logits)
    total = jnp.sum(expo, axis=1, keepdims=True)
    probs = expo / total
    lse = jnp.log(total)
    first = (picks[:, 0:1] == levels).astype(jnp.float32)
    second = (picks[:, 1:2] == levels).astype(jnp.float32)
    pfirst = jnp.sum(probs * first, axis=1, keepdims=True)
    psecond = jnp.sum(probs * second, axis=1, keepdims=True)
    denom = pfirst + psecond
    gfirst = pfirst / denom
    gsecond = psecond / denom
    cfirst = cotangent[:, 0:1]
    csecond = cotangent[:, 1:2]
    mixed = cfirst * gfirst + csecond * gsecond
    upward = (
        first * (cfirst - mixed) / denom
        + second * (csecond - mixed) / denom
        + balance_weight * load
    )
    inner = jnp.sum(probs * upward, axis=1, keepdims=True)
    grad = probs * (upward - inner) + 2.0 * zloss_weight * lse * probs
    return gfirst, gsecond, grad.astype(jnp.bfloat16)


def flip(index, mask, size):
    out = index
    bit = 1
    while bit < size:
        if mask & bit:
            out = out + bit * (1 - 2 * ((index // bit) % 2))
        bit *= 2
    return out


def exchange(
    n, d, capacity, owned,
    tok_hbm, w_hbm, cot_hbm, pick_hbm, slot_hbm,
    gates_hbm, wgrad_hbm, slots_hbm,
    tok_ref, w_ref, cot_ref, pick_ref, slot_ref, gates_ref, wgrad_ref, aux_rows, aux,
    lg_send, lg_recv, cnt_send, cnt_recv, own_grad, grads, rows_send, part_send, part_recv, own_wgrad, wgrads,
    in_sems, out_sems, cnt_ss, cnt_rs, lg_ss, lg_rs, gr_ss, gr_rs, a2a_ss, a2a_rs, rs_ss, rs_rs, ag_ss, ag_rs,
):
    me = lax.axis_index("mp")
    my_dp = lax.axis_index("dp")
    rows, feats = tok_ref.shape
    experts = w_ref.shape[0]
    own = rows // n
    half = own // 2
    width = owned * capacity
    eper = experts // d
    f32, bf16 = jnp.float32, jnp.bfloat16
    mp_order = list(range(n - 1, 0, -1))
    dp_order = list(range(d - 1, 0, -1))
    early = [k for k in (1, 2, 4) if k < n]
    late = [k for k in mp_order if k not in early]

    def to_mp(k):
        return {"dp": my_dp, "mp": flip(me, k, n)}

    def to_dp(k):
        return {"dp": flip(my_dp, k, d), "mp": me}

    tok_in = pltpu.make_async_copy(tok_hbm, tok_ref, in_sems.at[0])
    w_in = pltpu.make_async_copy(w_hbm, w_ref, in_sems.at[1])
    tok_in.start()
    w_in.start()
    small_in = [
        pltpu.make_async_copy(src, dst, in_sems.at[2 + i])
        for i, (src, dst) in enumerate(
            ((pick_hbm, pick_ref), (cot_hbm, cot_ref), (slot_hbm, slot_ref)))
    ]
    for copy in small_in:
        copy.start()
    barrier = pltpu.get_barrier_semaphore()
    for k in mp_order:
        pl.semaphore_signal(barrier, inc=1, device_id=to_mp(k), device_id_type=MESH)
    for k in dp_order:
        pl.semaphore_signal(barrier, inc=1, device_id=to_dp(k), device_id_type=MESH)

    for copy in small_in:
        copy.wait()
    picks = pick_ref[...]
    aux_rows[...] = jnp.zeros_like(aux_rows)
    aux_rows[0:2] = picks.astype(f32)
    aux_rows[2:4] = cot_ref[...]
    aux[...] = jnp.transpose(aux_rows[...])
    levels = lax.broadcasted_iota(jnp.int32, (experts, rows), 0)
    hot = (picks[0:1] == levels).astype(f32) + (picks[1:2] == levels).astype(f32)
    local = lax.dot_general(
        jnp.ones((8, rows), bf16), hot.astype(bf16), (((1,), (1,)), ((), ())), preferred_element_type=f32)
    cnt_send[...] = jnp.concatenate([local, local], axis=1)
    slots = slot_ref[...]
    owner_of = lax.div(picks, jnp.int32(owned))
    cell = jnp.where(slots >= 0, owner_of * width + slots * owned + picks - owner_of * owned, -1)
    place = lax.broadcasted_iota(jnp.int32, (width, rows), 0)

    w_in.wait()
    tok_in.wait()
    partial_value = lax.dot_general(
        tok_ref[...], w_ref[...], (((1,), (1,)), ((), ())), preferred_element_type=f32)
    for p in range(n):
        lo = partial_value[p * own : p * own + half]
        hi = partial_value[p * own + half : (p + 1) * own]
        lg_send[p] = jnp.concatenate([lo, hi], axis=1)

    pl.semaphore_wait(barrier, n - 1 + d - 1)

    lg = {}
    for k in mp_order:
        lg[k] = pltpu.make_async_remote_copy(
            src_ref=lg_send.at[flip(me, k, n)], dst_ref=lg_recv.at[k],
            send_sem=lg_ss.at[k], recv_sem=lg_rs.at[k], device_id=to_mp(k), device_id_type=MESH)
        lg[k].start()
    cnt = {}
    for k in dp_order:
        cnt[k] = pltpu.make_async_remote_copy(
            src_ref=cnt_send, dst_ref=cnt_recv.at[k],
            send_sem=cnt_ss.at[k], recv_sem=cnt_rs.at[k], device_id=to_dp(k), device_id_type=MESH)
        cnt[k].start()

    def fill(owner):
        target = place + owner * width
        onehot = ((cell[0:1] == target) | (cell[1:2] == target)).astype(f32).astype(bf16)
        return jnp.dot(onehot, tok_ref[...], preferred_element_type=f32).astype(bf16)

    columns = pl.ds(pl.multiple_of(me * feats, feats), feats)
    a2a = {}

    def push(k):
        a2a[k] = pltpu.make_async_remote_copy(
            src_ref=rows_send.at[k], dst_ref=slots_hbm.at[:, columns],
            send_sem=a2a_ss.at[k], recv_sem=a2a_rs.at[k], device_id=to_mp(k), device_id_type=MESH)
        a2a[k].start()

    for k in early:
        rows_send[k] = fill(flip(me, k, n))
        push(k)
    for k in late:
        rows_send[k] = fill(flip(me, k, n))

    for k in dp_order:
        cnt[k].wait()
    counts = cnt_send[...]
    for k in dp_order:
        counts = counts + cnt_recv[k]
    load = counts[0:1, :experts] * experts / (2.0 * rows * d)
    for k in mp_order:
        lg[k].wait()
    packed = lg_send[me]
    for k in mp_order:
        packed = packed + lg_recv[k]
    logits = jnp.concatenate([packed[:, :experts], packed[:, experts:]], axis=0)
    mine = pl.ds(pl.multiple_of(me * own, own), own)
    side = aux[mine, :]
    gfirst, gsecond, grad = route_grad(logits, side[:, 2:4], side[:, 0:2], load)
    own_grad[...] = grad
    grads[mine, :] = grad
    gr = {}
    for k in mp_order:
        gr[k] = pltpu.make_async_remote_copy(
            src_ref=own_grad, dst_ref=grads.at[mine, :],
            send_sem=gr_ss.at[k], recv_sem=gr_rs.at[k], device_id=to_mp(k), device_id_type=MESH)
        gr[k].start()
    rows_send[0] = fill(me)
    kept = pltpu.make_async_copy(rows_send.at[0], slots_hbm.at[:, columns], out_sems.at[0])
    kept.start()
    gates_ref[0:1] = jnp.transpose(jnp.broadcast_to(gfirst, (own, 128)))[0:1]
    gates_ref[1:2] = jnp.transpose(jnp.broadcast_to(gsecond, (own, 128)))[0:1]
    for k in mp_order:
        gr[k].wait()

    part = lax.dot_general(
        grads[...], tok_ref[...], (((0,), (0,)), ((), ())), preferred_element_type=f32)
    for j in range(d):
        part_send[j] = part[j * eper : (j + 1) * eper]
    rs = {}
    for k in dp_order:
        rs[k] = pltpu.make_async_remote_copy(
            src_ref=part_send.at[flip(my_dp, k, d)], dst_ref=part_recv.at[k],
            send_sem=rs_ss.at[k], recv_sem=rs_rs.at[k], device_id=to_dp(k), device_id_type=MESH)
        rs[k].start()
    for k in late:
        push(k)
    gates_out = pltpu.make_async_copy(gates_ref, gates_hbm, out_sems.at[1])
    gates_out.start()
    for k in dp_order:
        rs[k].wait()
    total = part_send[my_dp]
    for k in dp_order:
        total = total + part_recv[k]
    total = total.astype(bf16)
    own_wgrad[...] = total
    wgrads[my_dp] = total
    ag = {}
    for k in dp_order:
        ag[k] = pltpu.make_async_remote_copy(
            src_ref=own_wgrad, dst_ref=wgrads.at[my_dp],
            send_sem=ag_ss.at[k], recv_sem=ag_rs.at[k], device_id=to_dp(k), device_id_type=MESH)
        ag[k].start()
    for k in dp_order:
        ag[k].wait()
    for j in range(d):
        wgrad_ref[j * eper : (j + 1) * eper] = wgrads[j].astype(f32)
    wgrad_out = pltpu.make_async_copy(wgrad_ref, wgrad_hbm, out_sems.at[2])
    wgrad_out.start()
    for k in mp_order:
        a2a[k].wait()
    kept.wait()
    gates_out.wait()
    wgrad_out.wait()


def hand_out(pieces, gates_ref, wgrad_ref, slots_ref, gates_out, wgrad_out, slots_out, sems):
    size = slots_ref.shape[0] // pieces
    copies = [
        pltpu.make_async_copy(
            slots_ref.at[pl.ds(i * size, size)], slots_out.at[pl.ds(i * size, size)], sems.at[i])
        for i in range(pieces)
    ]
    copies.append(pltpu.make_async_copy(wgrad_ref, wgrad_out, sems.at[pieces]))
    copies.append(pltpu.make_async_copy(gates_ref, gates_out, sems.at[pieces + 1]))
    for copy in copies:
        copy.start()
    for copy in copies:
        copy.wait()


def on_device(n, d, tokens, router_weight, gate_cotangent, expert_index, slot_index):
    rows, feats = tokens.shape
    experts = router_weight.shape[1]
    own = rows // n
    capacity = 5 * rows // (2 * experts)
    owned = experts // n
    width = owned * capacity
    eper = experts // d
    bf16, f32 = jnp.bfloat16, jnp.float32
    dma = pltpu.SemaphoreType.DMA
    hbm = pl.BlockSpec(memory_space=pltpu.HBM)
    results = (
        jax.ShapeDtypeStruct((2, own), f32),
        jax.ShapeDtypeStruct((experts, feats), f32),
        jax.ShapeDtypeStruct((width, n * feats), bf16),
    )
    gates, wgrad, slotted = pl.pallas_call(
        functools.partial(exchange, n, d, capacity, owned),
        out_shape=results,
        in_specs=[hbm] * 5,
        out_specs=(hbm,) * 3,
        scratch_shapes=[
            pltpu.VMEM((rows, feats), bf16),
            pltpu.VMEM((experts, feats), bf16),
            pltpu.VMEM((2, rows), f32),
            pltpu.VMEM((2, rows), jnp.int32),
            pltpu.VMEM((2, rows), jnp.int32),
            pltpu.VMEM((2, own), f32),
            pltpu.VMEM((experts, feats), f32),
            pltpu.VMEM((8, rows), f32),
            pltpu.VMEM((rows, 8), f32),
            pltpu.VMEM((n, own // 2, 2 * experts), f32),
            pltpu.VMEM((n, own // 2, 2 * experts), f32),
            pltpu.VMEM((8, 2 * experts), f32),
            pltpu.VMEM((d, 8, 2 * experts), f32),
            pltpu.VMEM((own, experts), bf16),
            pltpu.VMEM((rows, experts), bf16),
            pltpu.VMEM((n, width, feats), bf16),
            pltpu.VMEM((d, eper, feats), f32),
            pltpu.VMEM((d, eper, feats), f32),
            pltpu.VMEM((eper, feats), bf16),
            pltpu.VMEM((d, eper, feats), bf16),
            dma((5,)), dma((3,)),
            dma((d,)), dma((d,)), dma((n,)), dma((n,)), dma((n,)), dma((n,)),
            dma((n,)), dma((n,)), dma((d,)), dma((d,)), dma((d,)), dma((d,)),
        ],
        compiler_params=pltpu.CompilerParams(
            collective_id=0, has_side_effects=True, vmem_limit_bytes=60 * 1024 * 1024
        ),
        name="exchange",
    )(tokens, router_weight.T, gate_cotangent.T, expert_index.T, slot_index.T)
    pieces = width // 16
    gates, wgrad, slotted = pl.pallas_call(
        functools.partial(hand_out, pieces),
        out_shape=results,
        in_specs=[hbm] * 3,
        out_specs=(hbm,) * 3,
        scratch_shapes=[dma((pieces + 2,))],
        compiler_params=pltpu.CompilerParams(vmem_limit_bytes=60 * 1024 * 1024),
        name="hand_out",
    )(gates, wgrad, slotted)
    dispatched = slotted.reshape(1, capacity, owned, n * feats).transpose(0, 2, 1, 3)
    return gates.T, wgrad.T, dispatched


def solution(mesh):
    n, d = mesh.shape["mp"], mesh.shape["dp"]
    in_specs = (P("dp", "mp"), P("mp", None), P("dp", None), P("dp", None), P("dp", None))
    out_specs = (P(("dp", "mp"), None), P("mp", None), P("dp", "mp", None, None))
    return jax.shard_map(
        functools.partial(on_device, n, d),
        mesh=mesh, in_specs=in_specs, out_specs=out_specs, check_vma=False,
    )
```

```python
import functools

import jax
import jax.numpy as jnp
from jax import lax
from jax.experimental import pallas as pl
from jax.experimental.pallas import tpu as pltpu
from jax.sharding import PartitionSpec as P

balance_weight = 0.5
zloss_weight = 0.02
MESH = pl.DeviceIdType.MESH


def route_grad(logits, cotangent, picks, load):
    levels = lax.broadcasted_iota(jnp.int32, logits.shape, 1).astype(jnp.float32)
    expo = jnp.exp(logits)
    total = jnp.sum(expo, axis=1, keepdims=True)
    probs = expo / total
    lse = jnp.log(total)
    first = (picks[:, 0:1] == levels).astype(jnp.float32)
    second = (picks[:, 1:2] == levels).astype(jnp.float32)
    pfirst = jnp.sum(probs * first, axis=1, keepdims=True)
    psecond = jnp.sum(probs * second, axis=1, keepdims=True)
    denom = pfirst + psecond
    gfirst = pfirst / denom
    gsecond = psecond / denom
    cfirst = cotangent[:, 0:1]
    csecond = cotangent[:, 1:2]
    mixed = cfirst * gfirst + csecond * gsecond
    upward = (
        first * (cfirst - mixed) / denom
        + second * (csecond - mixed) / denom
        + balance_weight * load
    )
    inner = jnp.sum(probs * upward, axis=1, keepdims=True)
    grad = probs * (upward - inner) + 2.0 * zloss_weight * lse * probs
    return gfirst, gsecond, grad.astype(jnp.bfloat16)


def flip(index, mask, size):
    out = index
    bit = 1
    while bit < size:
        if mask & bit:
            out = out + bit * (1 - 2 * ((index // bit) % 2))
        bit *= 2
    return out


def exchange(
    n, d, capacity, owned,
    tok_hbm, w_hbm, cot_hbm, pick_hbm, slot_hbm,
    gates_hbm, wgrad_hbm, slots_hbm,
    tok_ref, w_ref, cot_ref, pick_ref, slot_ref, gates_ref, wgrad_ref, aux_rows, aux,
    lg_send, lg_recv, cnt_send, cnt_recv, own_grad, grads, rows_send, part_send, part_recv, own_wgrad, wgrads,
    in_sems, out_sems, cnt_ss, cnt_rs, lg_ss, lg_rs, gr_ss, gr_rs, a2a_ss, a2a_rs, rs_ss, rs_rs, ag_ss, ag_rs,
):
    me = lax.axis_index("mp")
    my_dp = lax.axis_index("dp")
    rows, feats = tok_ref.shape
    experts = w_ref.shape[0]
    own = rows // n
    half = own // 2
    width = owned * capacity
    eper = experts // d
    f32, bf16 = jnp.float32, jnp.bfloat16
    mp_order = list(range(n - 1, 0, -1))
    dp_order = list(range(d - 1, 0, -1))
    early = [[k for k in batch if k < n] for batch in ((2, 4), (3, 5))]
    rest = [k for k in mp_order if not any(k in batch for batch in early)] + [0]
    late = [rest[i : i + 4] for i in range(0, len(rest), 4)]

    def to_mp(k):
        return {"dp": my_dp, "mp": flip(me, k, n)}

    def to_dp(k):
        return {"dp": flip(my_dp, k, d), "mp": me}

    tok_in = pltpu.make_async_copy(tok_hbm, tok_ref, in_sems.at[0])
    w_in = pltpu.make_async_copy(w_hbm, w_ref, in_sems.at[1])
    tok_in.start()
    w_in.start()
    small_in = [
        pltpu.make_async_copy(src, dst, in_sems.at[2 + i])
        for i, (src, dst) in enumerate(
            ((pick_hbm, pick_ref), (cot_hbm, cot_ref), (slot_hbm, slot_ref)))
    ]
    for copy in small_in:
        copy.start()
    barrier = pltpu.get_barrier_semaphore()
    for k in mp_order:
        pl.semaphore_signal(barrier, inc=1, device_id=to_mp(k), device_id_type=MESH)
    for k in dp_order:
        pl.semaphore_signal(barrier, inc=1, device_id=to_dp(k), device_id_type=MESH)

    for copy in small_in:
        copy.wait()
    picks = pick_ref[...]
    aux_rows[...] = jnp.zeros_like(aux_rows)
    aux_rows[0:2] = picks.astype(f32)
    aux_rows[2:4] = cot_ref[...]
    aux[...] = jnp.transpose(aux_rows[...])
    levels = lax.broadcasted_iota(jnp.int32, (experts, rows), 0)
    hot = (picks[0:1] == levels).astype(f32) + (picks[1:2] == levels).astype(f32)
    local = lax.dot_general(
        jnp.ones((8, rows), bf16), hot.astype(bf16), (((1,), (1,)), ((), ())), preferred_element_type=f32)
    cnt_send[...] = jnp.concatenate([local, local], axis=1)
    slots = slot_ref[...]
    owner_of = lax.div(picks, jnp.int32(owned))
    cell = jnp.where(slots >= 0, owner_of * width + slots * owned + picks - owner_of * owned, -1)
    place = lax.broadcasted_iota(jnp.int32, (width, rows), 0)

    w_in.wait()
    tok_in.wait()
    partial_value = lax.dot_general(
        tok_ref[...], w_ref[...], (((1,), (1,)), ((), ())), preferred_element_type=f32)
    for p in range(n):
        lo = partial_value[p * own : p * own + half]
        hi = partial_value[p * own + half : (p + 1) * own]
        lg_send[p] = jnp.concatenate([lo, hi], axis=1)

    pl.semaphore_wait(barrier, n - 1 + d - 1)

    lg = {}
    for k in mp_order:
        lg[k] = pltpu.make_async_remote_copy(
            src_ref=lg_send.at[flip(me, k, n)], dst_ref=lg_recv.at[k],
            send_sem=lg_ss.at[k], recv_sem=lg_rs.at[k], device_id=to_mp(k), device_id_type=MESH)
        lg[k].start()
    cnt = {}
    for k in dp_order:
        cnt[k] = pltpu.make_async_remote_copy(
            src_ref=cnt_send, dst_ref=cnt_recv.at[k],
            send_sem=cnt_ss.at[k], recv_sem=cnt_rs.at[k], device_id=to_dp(k), device_id_type=MESH)
        cnt[k].start()

    def fill(batch):
        onehots = []
        for k in batch:
            target = place + flip(me, k, n) * width
            onehots.append(((cell[0:1] == target) | (cell[1:2] == target)).astype(f32))
        onehot = jnp.concatenate(onehots, axis=0).astype(bf16)
        placed = jnp.dot(onehot, tok_ref[...], preferred_element_type=f32).astype(bf16)
        for i, k in enumerate(batch):
            rows_send[k] = placed[i * width : (i + 1) * width]

    columns = pl.ds(pl.multiple_of(me * feats, feats), feats)
    a2a = {}

    def push(k):
        a2a[k] = pltpu.make_async_remote_copy(
            src_ref=rows_send.at[k], dst_ref=slots_hbm.at[:, columns],
            send_sem=a2a_ss.at[k], recv_sem=a2a_rs.at[k], device_id=to_mp(k), device_id_type=MESH)
        a2a[k].start()

    for batch in early:
        fill(batch)
        for k in batch:
            push(k)

    for k in dp_order:
        cnt[k].wait()
    counts = cnt_send[...]
    for k in dp_order:
        counts = counts + cnt_recv[k]
    load = counts[0:1, :experts] * experts / (2.0 * rows * d)
    for k in mp_order:
        lg[k].wait()
    packed = lg_send[me]
    for k in mp_order:
        packed = packed + lg_recv[k]
    logits = jnp.concatenate([packed[:, :experts], packed[:, experts:]], axis=0)
    mine = pl.ds(pl.multiple_of(me * own, own), own)
    side = aux[mine, :]
    gfirst, gsecond, grad = route_grad(logits, side[:, 2:4], side[:, 0:2], load)
    own_grad[...] = grad
    grads[mine, :] = grad
    gr = {}
    for k in mp_order:
        gr[k] = pltpu.make_async_remote_copy(
            src_ref=own_grad, dst_ref=grads.at[mine, :],
            send_sem=gr_ss.at[k], recv_sem=gr_rs.at[k], device_id=to_mp(k), device_id_type=MESH)
        gr[k].start()
    for batch in late:
        fill(batch)
    kept = pltpu.make_async_copy(rows_send.at[0], slots_hbm.at[:, columns], out_sems.at[0])
    kept.start()
    gates_ref[0:1] = jnp.transpose(jnp.broadcast_to(gfirst, (own, 128)))[0:1]
    gates_ref[1:2] = jnp.transpose(jnp.broadcast_to(gsecond, (own, 128)))[0:1]
    for k in mp_order:
        gr[k].wait()

    part = lax.dot_general(
        grads[...], tok_ref[...], (((0,), (0,)), ((), ())), preferred_element_type=f32)
    for j in range(d):
        part_send[j] = part[j * eper : (j + 1) * eper]
    rs = {}
    for k in dp_order:
        rs[k] = pltpu.make_async_remote_copy(
            src_ref=part_send.at[flip(my_dp, k, d)], dst_ref=part_recv.at[k],
            send_sem=rs_ss.at[k], recv_sem=rs_rs.at[k], device_id=to_dp(k), device_id_type=MESH)
        rs[k].start()
    for batch in late:
        for k in batch:
            if k:
                push(k)
    gates_out = pltpu.make_async_copy(gates_ref, gates_hbm, out_sems.at[1])
    gates_out.start()
    for k in dp_order:
        rs[k].wait()
    total = part_send[my_dp]
    for k in dp_order:
        total = total + part_recv[k]
    total = total.astype(bf16)
    own_wgrad[...] = total
    wgrads[my_dp] = total
    ag = {}
    for k in dp_order:
        ag[k] = pltpu.make_async_remote_copy(
            src_ref=own_wgrad, dst_ref=wgrads.at[my_dp],
            send_sem=ag_ss.at[k], recv_sem=ag_rs.at[k], device_id=to_dp(k), device_id_type=MESH)
        ag[k].start()
    for k in dp_order:
        ag[k].wait()
    for j in range(d):
        wgrad_ref[j * eper : (j + 1) * eper] = wgrads[j].astype(f32)
    wgrad_out = pltpu.make_async_copy(wgrad_ref, wgrad_hbm, out_sems.at[2])
    wgrad_out.start()
    for k in mp_order:
        a2a[k].wait()
    kept.wait()
    gates_out.wait()
    wgrad_out.wait()


def hand_out(
    pieces, gates_ref, wgrad_ref, slots_ref, gates_out, wgrad_out, slots_out,
    gates_buf, wgrad_buf, slots_buf, in_sems, sems,
):
    size = slots_ref.shape[0] // pieces
    chunks = [pl.ds(i * size, size) for i in range(pieces)]
    routes = [(slots_ref.at[c], slots_buf.at[c], slots_out.at[c]) for c in chunks]
    routes.append((wgrad_ref, wgrad_buf, wgrad_out))
    routes.append((gates_ref, gates_buf, gates_out))
    ins = [pltpu.make_async_copy(a, b, in_sems.at[i]) for i, (a, b, _) in enumerate(routes)]
    outs = [pltpu.make_async_copy(b, c, sems.at[i]) for i, (_, b, c) in enumerate(routes)]
    for copy in ins:
        copy.start()
    for copy, out in zip(ins, outs):
        copy.wait()
        out.start()
    for out in outs:
        out.wait()


def on_device(n, d, tokens, router_weight, gate_cotangent, expert_index, slot_index):
    rows, feats = tokens.shape
    experts = router_weight.shape[1]
    own = rows // n
    capacity = 5 * rows // (2 * experts)
    owned = experts // n
    width = owned * capacity
    eper = experts // d
    bf16, f32 = jnp.bfloat16, jnp.float32
    dma = pltpu.SemaphoreType.DMA
    hbm = pl.BlockSpec(memory_space=pltpu.HBM)
    results = (
        jax.ShapeDtypeStruct((2, own), f32),
        jax.ShapeDtypeStruct((experts, feats), f32),
        jax.ShapeDtypeStruct((width, n * feats), bf16),
    )
    gates, wgrad, slotted = pl.pallas_call(
        functools.partial(exchange, n, d, capacity, owned),
        out_shape=results,
        in_specs=[hbm] * 5,
        out_specs=(hbm,) * 3,
        scratch_shapes=[
            pltpu.VMEM((rows, feats), bf16),
            pltpu.VMEM((experts, feats), bf16),
            pltpu.VMEM((2, rows), f32),
            pltpu.VMEM((2, rows), jnp.int32),
            pltpu.VMEM((2, rows), jnp.int32),
            pltpu.VMEM((2, own), f32),
            pltpu.VMEM((experts, feats), f32),
            pltpu.VMEM((8, rows), f32),
            pltpu.VMEM((rows, 8), f32),
            pltpu.VMEM((n, own // 2, 2 * experts), f32),
            pltpu.VMEM((n, own // 2, 2 * experts), f32),
            pltpu.VMEM((8, 2 * experts), f32),
            pltpu.VMEM((d, 8, 2 * experts), f32),
            pltpu.VMEM((own, experts), bf16),
            pltpu.VMEM((rows, experts), bf16),
            pltpu.VMEM((n, width, feats), bf16),
            pltpu.VMEM((d, eper, feats), f32),
            pltpu.VMEM((d, eper, feats), f32),
            pltpu.VMEM((eper, feats), bf16),
            pltpu.VMEM((d, eper, feats), bf16),
            dma((5,)), dma((3,)),
            dma((d,)), dma((d,)), dma((n,)), dma((n,)), dma((n,)), dma((n,)),
            dma((n,)), dma((n,)), dma((d,)), dma((d,)), dma((d,)), dma((d,)),
        ],
        compiler_params=pltpu.CompilerParams(
            collective_id=0, has_side_effects=True, vmem_limit_bytes=60 * 1024 * 1024
        ),
        name="exchange",
    )(tokens, router_weight.T, gate_cotangent.T, expert_index.T, slot_index.T)
    pieces = width // 16
    gates, wgrad, slotted = pl.pallas_call(
        functools.partial(hand_out, pieces),
        out_shape=results,
        in_specs=[hbm] * 3,
        out_specs=(hbm,) * 3,
        scratch_shapes=[
            pltpu.VMEM((2, own), f32),
            pltpu.VMEM((experts, feats), f32),
            pltpu.VMEM((width, n * feats), bf16),
            dma((pieces + 2,)), dma((pieces + 2,)),
        ],
        compiler_params=pltpu.CompilerParams(vmem_limit_bytes=60 * 1024 * 1024),
        name="hand_out",
    )(gates, wgrad, slotted)
    dispatched = slotted.reshape(1, capacity, owned, n * feats).transpose(0, 2, 1, 3)
    return gates.T, wgrad.T, dispatched


def solution(mesh):
    n, d = mesh.shape["mp"], mesh.shape["dp"]
    in_specs = (P("dp", "mp"), P("mp", None), P("dp", None), P("dp", None), P("dp", None))
    out_specs = (P(("dp", "mp"), None), P("mp", None), P("dp", "mp", None, None))
    return jax.shard_map(
        functools.partial(on_device, n, d),
        mesh=mesh, in_specs=in_specs, out_specs=out_specs, check_vma=False,
    )
```

```python
import functools

import jax
import jax.numpy as jnp
from jax import lax
from jax.experimental import pallas as pl
from jax.experimental.pallas import tpu as pltpu
from jax.sharding import PartitionSpec as P

balance_weight = 0.5
zloss_weight = 0.02
MESH = pl.DeviceIdType.MESH


def route_grad(logits, cotangent, picks, load):
    levels = lax.broadcasted_iota(jnp.int32, logits.shape, 1).astype(jnp.float32)
    expo = jnp.exp(logits)
    total = jnp.sum(expo, axis=1, keepdims=True)
    probs = expo / total
    lse = jnp.log(total)
    first = (picks[:, 0:1] == levels).astype(jnp.float32)
    second = (picks[:, 1:2] == levels).astype(jnp.float32)
    pfirst = jnp.sum(probs * first, axis=1, keepdims=True)
    psecond = jnp.sum(probs * second, axis=1, keepdims=True)
    denom = pfirst + psecond
    gfirst = pfirst / denom
    gsecond = psecond / denom
    cfirst = cotangent[:, 0:1]
    csecond = cotangent[:, 1:2]
    mixed = cfirst * gfirst + csecond * gsecond
    upward = (
        first * (cfirst - mixed) / denom
        + second * (csecond - mixed) / denom
        + balance_weight * load
    )
    inner = jnp.sum(probs * upward, axis=1, keepdims=True)
    grad = probs * (upward - inner) + 2.0 * zloss_weight * lse * probs
    return gfirst, gsecond, grad.astype(jnp.bfloat16)


def flip(index, mask, size):
    out = index
    bit = 1
    while bit < size:
        if mask & bit:
            out = out + bit * (1 - 2 * ((index // bit) % 2))
        bit *= 2
    return out


def exchange(
    n, d, capacity, owned,
    tok_hbm, w_hbm, cot_hbm, pick_hbm, slot_hbm,
    gates_hbm, wgrad_hbm, slots_hbm,
    tok_ref, w_ref, cot_ref, pick_ref, slot_ref, gates_ref, wgrad_ref, aux_rows, aux,
    lg_send, lg_recv, cnt_send, cnt_recv, own_grad, grads, rows_send, part_send, part_recv, own_wgrad, wgrads,
    in_sems, out_sems, cnt_ss, cnt_rs, lg_ss, lg_rs, gr_ss, gr_rs, a2a_ss, a2a_rs, rs_ss, rs_rs, ag_ss, ag_rs,
):
    me = lax.axis_index("mp")
    my_dp = lax.axis_index("dp")
    rows, feats = tok_ref.shape
    experts = w_ref.shape[0]
    own = rows // n
    half = own // 2
    width = owned * capacity
    eper = experts // d
    f32, bf16 = jnp.float32, jnp.bfloat16
    mp_order = list(range(n - 1, 0, -1))
    dp_order = list(range(d - 1, 0, -1))
    early, middle = [[k for k in batch if k < n] for batch in ((1, 0), (2, 4))]
    rest = [k for k in mp_order if k not in early + middle]
    late = [rest[i : i + 4] for i in range(0, len(rest), 4)]
    halves = part_send.shape[0]
    wide = feats // halves
    cuts = tok_ref.shape[0] // 2

    def to_mp(k):
        return {"dp": my_dp, "mp": flip(me, k, n)}

    def to_dp(k):
        return {"dp": flip(my_dp, k, d), "mp": me}

    w_in = pltpu.make_async_copy(w_hbm, w_ref, in_sems.at[1])
    w_in.start()
    tok_in = [
        pltpu.make_async_copy(
            tok_hbm.at[i * cuts : (i + 1) * cuts], tok_ref.at[i * cuts : (i + 1) * cuts],
            in_sems.at[5 * i])
        for i in range(2)
    ]
    for copy in tok_in:
        copy.start()
    small_in = [
        pltpu.make_async_copy(src, dst, in_sems.at[2 + i])
        for i, (src, dst) in enumerate(
            ((pick_hbm, pick_ref), (cot_hbm, cot_ref), (slot_hbm, slot_ref)))
    ]
    for copy in small_in:
        copy.start()
    barrier = pltpu.get_barrier_semaphore()
    for k in mp_order:
        pl.semaphore_signal(barrier, inc=1, device_id=to_mp(k), device_id_type=MESH)
    for k in dp_order:
        pl.semaphore_signal(barrier, inc=1, device_id=to_dp(k), device_id_type=MESH)

    for copy in small_in:
        copy.wait()
    picks = pick_ref[...]
    aux_rows[...] = jnp.zeros_like(aux_rows)
    aux_rows[0:2] = picks.astype(f32)
    aux_rows[2:4] = cot_ref[...]
    aux[...] = jnp.transpose(aux_rows[...])
    levels = lax.broadcasted_iota(jnp.int32, (experts, rows), 0)
    hot = (picks[0:1] == levels).astype(f32) + (picks[1:2] == levels).astype(f32)
    local = lax.dot_general(
        jnp.ones((8, rows), bf16), hot.astype(bf16), (((1,), (1,)), ((), ())), preferred_element_type=f32)
    cnt_send[...] = jnp.concatenate([local, local], axis=1)
    slots = slot_ref[...]
    owner_of = lax.div(picks, jnp.int32(owned))
    cell = jnp.where(slots >= 0, owner_of * width + slots * owned + picks - owner_of * owned, -1)
    place = lax.broadcasted_iota(jnp.int32, (width, rows), 0)

    w_in.wait()
    for i, copy in enumerate(tok_in):
        copy.wait()
        partial_value = lax.dot_general(
            tok_ref[i * cuts : (i + 1) * cuts], w_ref[...], (((1,), (1,)), ((), ())),
            preferred_element_type=f32)
        for p in range(n // 2):
            lo = partial_value[p * own : p * own + half]
            hi = partial_value[p * own + half : (p + 1) * own]
            lg_send[i * (n // 2) + p] = jnp.concatenate([lo, hi], axis=1)

    pl.semaphore_wait(barrier, n - 1 + d - 1)

    lg = {}
    for k in mp_order:
        lg[k] = pltpu.make_async_remote_copy(
            src_ref=lg_send.at[flip(me, k, n)], dst_ref=lg_recv.at[k],
            send_sem=lg_ss.at[k], recv_sem=lg_rs.at[k], device_id=to_mp(k), device_id_type=MESH)
        lg[k].start()
    cnt = {}
    for k in dp_order:
        cnt[k] = pltpu.make_async_remote_copy(
            src_ref=cnt_send, dst_ref=cnt_recv.at[k],
            send_sem=cnt_ss.at[k], recv_sem=cnt_rs.at[k], device_id=to_dp(k), device_id_type=MESH)
        cnt[k].start()

    def fill(batch):
        onehots = []
        for k in batch:
            target = place + flip(me, k, n) * width
            onehots.append(((cell[0:1] == target) | (cell[1:2] == target)).astype(f32))
        onehot = jnp.concatenate(onehots, axis=0).astype(bf16)
        placed = jnp.dot(onehot, tok_ref[...], preferred_element_type=f32).astype(bf16)
        for i, k in enumerate(batch):
            rows_send[k] = placed[i * width : (i + 1) * width]

    columns = pl.ds(pl.multiple_of(me * feats, feats), feats)
    a2a = {}

    def push(k):
        a2a[k] = pltpu.make_async_remote_copy(
            src_ref=rows_send.at[k], dst_ref=slots_hbm.at[:, columns],
            send_sem=a2a_ss.at[k], recv_sem=a2a_rs.at[k], device_id=to_mp(k), device_id_type=MESH)
        a2a[k].start()

    fill(early)
    for k in early:
        if k:
            push(k)
    kept = pltpu.make_async_copy(rows_send.at[0], slots_hbm.at[:, columns], out_sems.at[0])
    kept.start()
    if middle:
        fill(middle)

    for k in dp_order:
        cnt[k].wait()
    counts = cnt_send[...]
    for k in dp_order:
        counts = counts + cnt_recv[k]
    load = counts[0:1, :experts] * experts / (2.0 * rows * d)
    for k in mp_order:
        lg[k].wait()
    packed = lg_send[me]
    for k in mp_order:
        packed = packed + lg_recv[k]
    logits = jnp.concatenate([packed[:, :experts], packed[:, experts:]], axis=0)
    mine = pl.ds(pl.multiple_of(me * own, own), own)
    side = aux[mine, :]
    gfirst, gsecond, grad = route_grad(logits, side[:, 2:4], side[:, 0:2], load)
    own_grad[...] = grad
    grads[mine, :] = grad
    gr = {}
    for k in mp_order:
        gr[k] = pltpu.make_async_remote_copy(
            src_ref=own_grad, dst_ref=grads.at[mine, :],
            send_sem=gr_ss.at[k], recv_sem=gr_rs.at[k], device_id=to_mp(k), device_id_type=MESH)
        gr[k].start()
    for k in middle:
        push(k)
    for batch in late:
        fill(batch)
    gates_ref[0:1] = jnp.transpose(jnp.broadcast_to(gfirst, (own, 128)))[0:1]
    gates_ref[1:2] = jnp.transpose(jnp.broadcast_to(gsecond, (own, 128)))[0:1]
    for k in mp_order:
        gr[k].wait()

    rs, ag = {}, {}
    for h in range(halves):
        part = lax.dot_general(
            grads[...], tok_ref[:, h * wide : (h + 1) * wide], (((0,), (0,)), ((), ())),
            preferred_element_type=f32)
        for j in range(d):
            part_send[h, j] = part[j * eper : (j + 1) * eper]
        for k in dp_order:
            rs[h, k] = pltpu.make_async_remote_copy(
                src_ref=part_send.at[h, flip(my_dp, k, d)], dst_ref=part_recv.at[h, k],
                send_sem=rs_ss.at[h, k], recv_sem=rs_rs.at[h, k],
                device_id=to_dp(k), device_id_type=MESH)
            rs[h, k].start()
    for batch in late:
        for k in batch:
            push(k)
    gates_out = pltpu.make_async_copy(gates_ref, gates_hbm, out_sems.at[1])
    gates_out.start()
    for h in range(halves):
        for k in dp_order:
            rs[h, k].wait()
        total = part_send[h, my_dp]
        for k in dp_order:
            total = total + part_recv[h, k]
        total = total.astype(bf16)
        own_wgrad[h] = total
        wgrads[h, my_dp] = total
        for k in dp_order:
            ag[h, k] = pltpu.make_async_remote_copy(
                src_ref=own_wgrad.at[h], dst_ref=wgrads.at[h, my_dp],
                send_sem=ag_ss.at[h, k], recv_sem=ag_rs.at[h, k],
                device_id=to_dp(k), device_id_type=MESH)
            ag[h, k].start()
    for h in range(halves):
        for k in dp_order:
            ag[h, k].wait()
        for j in range(d):
            wgrad_ref[j * eper : (j + 1) * eper, h * wide : (h + 1) * wide] = wgrads[h, j].astype(f32)
    wgrad_out = pltpu.make_async_copy(wgrad_ref, wgrad_hbm, out_sems.at[2])
    wgrad_out.start()
    for k in mp_order:
        a2a[k].wait()
    kept.wait()
    gates_out.wait()
    wgrad_out.wait()


def hand_out(
    pieces, gates_ref, wgrad_ref, slots_ref, gates_out, wgrad_out, slots_out,
    gates_buf, wgrad_buf, slots_buf, in_sems, sems,
):
    size = slots_ref.shape[0] // pieces
    chunks = [pl.ds(i * size, size) for i in range(pieces)]
    routes = [(slots_ref.at[c], slots_buf.at[c], slots_out.at[c]) for c in chunks]
    routes.append((wgrad_ref, wgrad_buf, wgrad_out))
    routes.append((gates_ref, gates_buf, gates_out))
    ins = [pltpu.make_async_copy(a, b, in_sems.at[i]) for i, (a, b, _) in enumerate(routes)]
    outs = [pltpu.make_async_copy(b, c, sems.at[i]) for i, (_, b, c) in enumerate(routes)]
    for copy in ins:
        copy.start()
    for copy, out in zip(ins, outs):
        copy.wait()
        out.start()
    for out in outs:
        out.wait()


def on_device(n, d, tokens, router_weight, gate_cotangent, expert_index, slot_index):
    rows, feats = tokens.shape
    experts = router_weight.shape[1]
    own = rows // n
    capacity = 5 * rows // (2 * experts)
    owned = experts // n
    width = owned * capacity
    eper = experts // d
    halves = 2
    bf16, f32 = jnp.bfloat16, jnp.float32
    dma = pltpu.SemaphoreType.DMA
    hbm = pl.BlockSpec(memory_space=pltpu.HBM)
    results = (
        jax.ShapeDtypeStruct((2, own), f32),
        jax.ShapeDtypeStruct((experts, feats), f32),
        jax.ShapeDtypeStruct((width, n * feats), bf16),
    )
    gates, wgrad, slotted = pl.pallas_call(
        functools.partial(exchange, n, d, capacity, owned),
        out_shape=results,
        in_specs=[hbm] * 5,
        out_specs=(hbm,) * 3,
        scratch_shapes=[
            pltpu.VMEM((rows, feats), bf16),
            pltpu.VMEM((experts, feats), bf16),
            pltpu.VMEM((2, rows), f32),
            pltpu.VMEM((2, rows), jnp.int32),
            pltpu.VMEM((2, rows), jnp.int32),
            pltpu.VMEM((2, own), f32),
            pltpu.VMEM((experts, feats), f32),
            pltpu.VMEM((8, rows), f32),
            pltpu.VMEM((rows, 8), f32),
            pltpu.VMEM((n, own // 2, 2 * experts), f32),
            pltpu.VMEM((n, own // 2, 2 * experts), f32),
            pltpu.VMEM((8, 2 * experts), f32),
            pltpu.VMEM((d, 8, 2 * experts), f32),
            pltpu.VMEM((own, experts), bf16),
            pltpu.VMEM((rows, experts), bf16),
            pltpu.VMEM((n, width, feats), bf16),
            pltpu.VMEM((halves, d, eper, feats // halves), f32),
            pltpu.VMEM((halves, d, eper, feats // halves), f32),
            pltpu.VMEM((halves, eper, feats // halves), bf16),
            pltpu.VMEM((halves, d, eper, feats // halves), bf16),
            dma((6,)), dma((3,)),
            dma((d,)), dma((d,)), dma((n,)), dma((n,)), dma((n,)), dma((n,)),
            dma((n,)), dma((n,)), dma((halves, d)), dma((halves, d)), dma((halves, d)), dma((halves, d)),
        ],
        compiler_params=pltpu.CompilerParams(
            collective_id=0, has_side_effects=True, vmem_limit_bytes=60 * 1024 * 1024
        ),
        name="exchange",
    )(tokens, router_weight.T, gate_cotangent.T, expert_index.T, slot_index.T)
    pieces = width // 16
    gates, wgrad, slotted = pl.pallas_call(
        functools.partial(hand_out, pieces),
        out_shape=results,
        in_specs=[hbm] * 3,
        out_specs=(hbm,) * 3,
        scratch_shapes=[
            pltpu.VMEM((2, own), f32),
            pltpu.VMEM((experts, feats), f32),
            pltpu.VMEM((width, n * feats), bf16),
            dma((pieces + 2,)), dma((pieces + 2,)),
        ],
        compiler_params=pltpu.CompilerParams(vmem_limit_bytes=60 * 1024 * 1024),
        name="hand_out",
    )(gates, wgrad, slotted)
    dispatched = slotted.reshape(1, capacity, owned, n * feats).transpose(0, 2, 1, 3)
    return gates.T, wgrad.T, dispatched


def solution(mesh):
    n, d = mesh.shape["mp"], mesh.shape["dp"]
    in_specs = (P("dp", "mp"), P("mp", None), P("dp", None), P("dp", None), P("dp", None))
    out_specs = (P(("dp", "mp"), None), P("mp", None), P("dp", "mp", None, None))
    return jax.shard_map(
        functools.partial(on_device, n, d),
        mesh=mesh, in_specs=in_specs, out_specs=out_specs, check_vma=False,
    )
```

```python
import functools

import jax
import jax.numpy as jnp
from jax import lax
from jax.experimental import pallas as pl
from jax.experimental.pallas import tpu as pltpu
from jax.sharding import PartitionSpec as P

balance_weight = 0.5
zloss_weight = 0.02
MESH = pl.DeviceIdType.MESH


def route_grad(logits, cotangent, picks, load):
    levels = lax.broadcasted_iota(jnp.int32, logits.shape, 1).astype(jnp.float32)
    expo = jnp.exp(logits)
    total = jnp.sum(expo, axis=1, keepdims=True)
    probs = expo / total
    lse = jnp.log(total)
    first = (picks[:, 0:1] == levels).astype(jnp.float32)
    second = (picks[:, 1:2] == levels).astype(jnp.float32)
    pfirst = jnp.sum(probs * first, axis=1, keepdims=True)
    psecond = jnp.sum(probs * second, axis=1, keepdims=True)
    denom = pfirst + psecond
    gfirst = pfirst / denom
    gsecond = psecond / denom
    cfirst = cotangent[:, 0:1]
    csecond = cotangent[:, 1:2]
    mixed = cfirst * gfirst + csecond * gsecond
    upward = (
        first * (cfirst - mixed) / denom
        + second * (csecond - mixed) / denom
        + balance_weight * load
    )
    inner = jnp.sum(probs * upward, axis=1, keepdims=True)
    grad = probs * (upward - inner) + 2.0 * zloss_weight * lse * probs
    return gfirst, gsecond, grad.astype(jnp.bfloat16)


def flip(index, mask, size):
    out = index
    bit = 1
    while bit < size:
        if mask & bit:
            out = out + bit * (1 - 2 * ((index // bit) % 2))
        bit *= 2
    return out


def exchange(
    n, d, capacity, owned,
    tok_hbm, w_hbm, cot_hbm, pick_hbm, slot_hbm,
    gates_ref, wgrad_ref, slots_ref,
    tok_ref, w_ref, cot_ref, pick_ref, slot_ref, aux_rows, aux,
    lg_send, lg_recv, cnt_send, cnt_recv, own_grad, grads, rows_send, part_send, part_recv, own_wgrad, wgrads,
    in_sems, out_sems, cnt_ss, cnt_rs, lg_ss, lg_rs, gr_ss, gr_rs, a2a_ss, a2a_rs, rs_ss, rs_rs, ag_ss, ag_rs,
):
    me = lax.axis_index("mp")
    my_dp = lax.axis_index("dp")
    rows, feats = tok_ref.shape
    experts = w_ref.shape[0]
    own = rows // n
    half = own // 2
    width = owned * capacity
    eper = experts // d
    f32, bf16 = jnp.float32, jnp.bfloat16
    mp_order = list(range(n - 1, 0, -1))
    dp_order = list(range(d - 1, 0, -1))
    early = [k for k in (1, 2, 4, 0) if k < n]
    middle = [k for k in mp_order if k not in early][:2]
    rest = [k for k in mp_order if k not in early + middle]
    late = [rest[i : i + 4] for i in range(0, len(rest), 4)]
    halves = part_send.shape[0]
    wide = feats // halves
    cuts = tok_ref.shape[0] // 2

    def to_mp(k):
        return {"dp": my_dp, "mp": flip(me, k, n)}

    def to_dp(k):
        return {"dp": flip(my_dp, k, d), "mp": me}

    w_in = pltpu.make_async_copy(w_hbm, w_ref, in_sems.at[1])
    w_in.start()
    tok_in = [
        pltpu.make_async_copy(
            tok_hbm.at[i * cuts : (i + 1) * cuts], tok_ref.at[i * cuts : (i + 1) * cuts],
            in_sems.at[5 * i])
        for i in range(2)
    ]
    for copy in tok_in:
        copy.start()
    small_in = [
        pltpu.make_async_copy(src, dst, in_sems.at[2 + i])
        for i, (src, dst) in enumerate(
            ((pick_hbm, pick_ref), (cot_hbm, cot_ref), (slot_hbm, slot_ref)))
    ]
    for copy in small_in:
        copy.start()
    barrier = pltpu.get_barrier_semaphore()
    for k in mp_order:
        pl.semaphore_signal(barrier, inc=1, device_id=to_mp(k), device_id_type=MESH)
    for k in dp_order:
        pl.semaphore_signal(barrier, inc=1, device_id=to_dp(k), device_id_type=MESH)

    for copy in small_in:
        copy.wait()
    picks = pick_ref[...]
    aux_rows[...] = jnp.zeros_like(aux_rows)
    aux_rows[0:2] = picks.astype(f32)
    aux_rows[2:4] = cot_ref[...]
    aux[...] = jnp.transpose(aux_rows[...])
    levels = lax.broadcasted_iota(jnp.int32, (experts, rows), 0)
    hot = (picks[0:1] == levels).astype(f32) + (picks[1:2] == levels).astype(f32)
    local = lax.dot_general(
        jnp.ones((8, rows), bf16), hot.astype(bf16), (((1,), (1,)), ((), ())), preferred_element_type=f32)
    cnt_send[...] = jnp.concatenate([local, local], axis=1)
    slots = slot_ref[...]
    owner_of = lax.div(picks, jnp.int32(owned))
    cell = jnp.where(slots >= 0, owner_of * width + slots * owned + picks - owner_of * owned, -1)
    place = lax.broadcasted_iota(jnp.int32, (width, rows), 0)

    w_in.wait()
    for i, copy in enumerate(tok_in):
        copy.wait()
        partial_value = lax.dot_general(
            tok_ref[i * cuts : (i + 1) * cuts], w_ref[...], (((1,), (1,)), ((), ())),
            preferred_element_type=f32)
        for p in range(n // 2):
            lo = partial_value[p * own : p * own + half]
            hi = partial_value[p * own + half : (p + 1) * own]
            lg_send[i * (n // 2) + p] = jnp.concatenate([lo, hi], axis=1)

    pl.semaphore_wait(barrier, n - 1 + d - 1)

    lg = {}
    for k in mp_order:
        lg[k] = pltpu.make_async_remote_copy(
            src_ref=lg_send.at[flip(me, k, n)], dst_ref=lg_recv.at[k],
            send_sem=lg_ss.at[k], recv_sem=lg_rs.at[k], device_id=to_mp(k), device_id_type=MESH)
        lg[k].start()
    cnt = {}
    for k in dp_order:
        cnt[k] = pltpu.make_async_remote_copy(
            src_ref=cnt_send, dst_ref=cnt_recv.at[k],
            send_sem=cnt_ss.at[k], recv_sem=cnt_rs.at[k], device_id=to_dp(k), device_id_type=MESH)
        cnt[k].start()

    def fill(batch):
        onehots = []
        for k in batch:
            target = place + flip(me, k, n) * width
            onehots.append(((cell[0:1] == target) | (cell[1:2] == target)).astype(f32))
        onehot = jnp.concatenate(onehots, axis=0).astype(bf16)
        placed = jnp.dot(onehot, tok_ref[...], preferred_element_type=f32).astype(bf16)
        for i, k in enumerate(batch):
            rows_send[k] = placed[i * width : (i + 1) * width]

    columns = pl.ds(pl.multiple_of(me * feats, feats), feats)
    a2a = {}

    def push(k):
        a2a[k] = pltpu.make_async_remote_copy(
            src_ref=rows_send.at[k], dst_ref=slots_ref.at[:, columns],
            send_sem=a2a_ss.at[k], recv_sem=a2a_rs.at[k], device_id=to_mp(k), device_id_type=MESH)
        a2a[k].start()

    fill(early)
    for k in early:
        if k:
            push(k)
    kept = pltpu.make_async_copy(rows_send.at[0], slots_ref.at[:, columns], out_sems.at[0])
    kept.start()

    for k in dp_order:
        cnt[k].wait()
    counts = cnt_send[...]
    for k in dp_order:
        counts = counts + cnt_recv[k]
    load = counts[0:1, :experts] * experts / (2.0 * rows * d)
    for k in mp_order:
        lg[k].wait()
    packed = lg_send[me]
    for k in mp_order:
        packed = packed + lg_recv[k]
    logits = jnp.concatenate([packed[:, :experts], packed[:, experts:]], axis=0)
    mine = pl.ds(pl.multiple_of(me * own, own), own)
    side = aux[mine, :]
    gfirst, gsecond, grad = route_grad(logits, side[:, 2:4], side[:, 0:2], load)
    own_grad[...] = grad
    grads[mine, :] = grad
    gr = {}
    for k in mp_order:
        gr[k] = pltpu.make_async_remote_copy(
            src_ref=own_grad, dst_ref=grads.at[mine, :],
            send_sem=gr_ss.at[k], recv_sem=gr_rs.at[k], device_id=to_mp(k), device_id_type=MESH)
        gr[k].start()
    for batch in [middle] + late:
        if batch:
            fill(batch)
    gates_ref[0:1] = jnp.transpose(jnp.broadcast_to(gfirst, (own, 128)))[0:1]
    gates_ref[1:2] = jnp.transpose(jnp.broadcast_to(gsecond, (own, 128)))[0:1]
    for k in mp_order:
        gr[k].wait()
    for k in middle:
        push(k)

    rs, ag = {}, {}
    for h in range(halves):
        part = lax.dot_general(
            grads[...], tok_ref[:, h * wide : (h + 1) * wide], (((0,), (0,)), ((), ())),
            preferred_element_type=f32)
        for j in range(d):
            part_send[h, j] = part[j * eper : (j + 1) * eper]
        for k in dp_order:
            rs[h, k] = pltpu.make_async_remote_copy(
                src_ref=part_send.at[h, flip(my_dp, k, d)], dst_ref=part_recv.at[h, k],
                send_sem=rs_ss.at[h, k], recv_sem=rs_rs.at[h, k],
                device_id=to_dp(k), device_id_type=MESH)
            rs[h, k].start()
    for batch in late:
        for k in batch:
            push(k)
    for h in range(halves):
        for k in dp_order:
            rs[h, k].wait()
        total = part_send[h, my_dp]
        for k in dp_order:
            total = total + part_recv[h, k]
        total = total.astype(bf16)
        own_wgrad[h] = total
        wgrads[h, my_dp] = total
        for k in dp_order:
            ag[h, k] = pltpu.make_async_remote_copy(
                src_ref=own_wgrad.at[h], dst_ref=wgrads.at[h, my_dp],
                send_sem=ag_ss.at[h, k], recv_sem=ag_rs.at[h, k],
                device_id=to_dp(k), device_id_type=MESH)
            ag[h, k].start()
    for h in range(halves):
        for k in dp_order:
            ag[h, k].wait()
        for j in range(d):
            wgrad_ref[j * eper : (j + 1) * eper, h * wide : (h + 1) * wide] = wgrads[h, j].astype(f32)
    for k in mp_order:
        a2a[k].wait()
    kept.wait()


def hand_out(pieces, gates_ref, wgrad_ref, slots_ref, gates_out, wgrad_out, slots_out, sems):
    size = slots_ref.shape[0] // pieces
    chunks = [pl.ds(i * size, size) for i in range(pieces)]
    routes = [(slots_ref.at[c], slots_out.at[c]) for c in chunks]
    routes += [(wgrad_ref, wgrad_out), (gates_ref, gates_out)]
    copies = [pltpu.make_async_copy(a, b, sems.at[i]) for i, (a, b) in enumerate(routes)]
    for copy in copies:
        copy.start()
    for copy in copies:
        copy.wait()


def on_device(n, d, tokens, router_weight, gate_cotangent, expert_index, slot_index):
    rows, feats = tokens.shape
    experts = router_weight.shape[1]
    own = rows // n
    capacity = 5 * rows // (2 * experts)
    owned = experts // n
    width = owned * capacity
    eper = experts // d
    halves = 2
    bf16, f32 = jnp.bfloat16, jnp.float32
    dma = pltpu.SemaphoreType.DMA
    vmem = pl.BlockSpec(memory_space=pltpu.VMEM)
    hbm = pl.BlockSpec(memory_space=pltpu.HBM)
    results = (
        jax.ShapeDtypeStruct((2, own), f32),
        jax.ShapeDtypeStruct((experts, feats), f32),
        jax.ShapeDtypeStruct((width, n * feats), bf16),
    )
    gates, wgrad, slotted = pl.pallas_call(
        functools.partial(exchange, n, d, capacity, owned),
        out_shape=results,
        in_specs=[hbm] * 5,
        out_specs=(vmem,) * 3,
        scratch_shapes=[
            pltpu.VMEM((rows, feats), bf16),
            pltpu.VMEM((experts, feats), bf16),
            pltpu.VMEM((2, rows), f32),
            pltpu.VMEM((2, rows), jnp.int32),
            pltpu.VMEM((2, rows), jnp.int32),
            pltpu.VMEM((8, rows), f32),
            pltpu.VMEM((rows, 8), f32),
            pltpu.VMEM((n, own // 2, 2 * experts), f32),
            pltpu.VMEM((n, own // 2, 2 * experts), f32),
            pltpu.VMEM((8, 2 * experts), f32),
            pltpu.VMEM((d, 8, 2 * experts), f32),
            pltpu.VMEM((own, experts), bf16),
            pltpu.VMEM((rows, experts), bf16),
            pltpu.VMEM((n, width, feats), bf16),
            pltpu.VMEM((halves, d, eper, feats // halves), f32),
            pltpu.VMEM((halves, d, eper, feats // halves), f32),
            pltpu.VMEM((halves, eper, feats // halves), bf16),
            pltpu.VMEM((halves, d, eper, feats // halves), bf16),
            dma((6,)), dma((1,)),
            dma((d,)), dma((d,)), dma((n,)), dma((n,)), dma((n,)), dma((n,)),
            dma((n,)), dma((n,)), dma((halves, d)), dma((halves, d)), dma((halves, d)), dma((halves, d)),
        ],
        compiler_params=pltpu.CompilerParams(
            collective_id=0, has_side_effects=True, vmem_limit_bytes=24 * 1024 * 1024
        ),
        name="exchange",
    )(*[
        pltpu.with_memory_space_constraint(x, pltpu.HBM)
        for x in (tokens, router_weight.T, gate_cotangent.T, expert_index.T, slot_index.T)
    ])
    pieces = width // 16
    gates, wgrad, slotted = pl.pallas_call(
        functools.partial(hand_out, pieces),
        out_shape=results,
        in_specs=[vmem] * 3,
        out_specs=(hbm,) * 3,
        scratch_shapes=[dma((pieces + 2,))],
        compiler_params=pltpu.CompilerParams(vmem_limit_bytes=16 * 1024 * 1024),
        name="hand_out",
    )(gates, wgrad, slotted)
    dispatched = slotted.reshape(1, capacity, owned, n * feats).transpose(0, 2, 1, 3)
    return gates.T, wgrad.T, dispatched


def solution(mesh):
    n, d = mesh.shape["mp"], mesh.shape["dp"]
    in_specs = (P("dp", "mp"), P("mp", None), P("dp", None), P("dp", None), P("dp", None))
    out_specs = (P(("dp", "mp"), None), P("mp", None), P("dp", "mp", None, None))
    return jax.shard_map(
        functools.partial(on_device, n, d),
        mesh=mesh, in_specs=in_specs, out_specs=out_specs, check_vma=False,
    )
```

```python
import functools

import jax
import jax.numpy as jnp
from jax import lax
from jax.experimental import pallas as pl
from jax.experimental.pallas import tpu as pltpu
from jax.sharding import PartitionSpec as P

balance_weight = 0.5
zloss_weight = 0.02
MESH = pl.DeviceIdType.MESH


def route_grad(logits, cotangent, picks, load):
    levels = lax.broadcasted_iota(jnp.int32, logits.shape, 1).astype(jnp.float32)
    expo = jnp.exp(logits)
    total = jnp.sum(expo, axis=1, keepdims=True)
    probs = expo / total
    lse = jnp.log(total)
    first = (picks[:, 0:1] == levels).astype(jnp.float32)
    second = (picks[:, 1:2] == levels).astype(jnp.float32)
    pfirst = jnp.sum(probs * first, axis=1, keepdims=True)
    psecond = jnp.sum(probs * second, axis=1, keepdims=True)
    denom = pfirst + psecond
    gfirst = pfirst / denom
    gsecond = psecond / denom
    cfirst = cotangent[:, 0:1]
    csecond = cotangent[:, 1:2]
    mixed = cfirst * gfirst + csecond * gsecond
    upward = (
        first * (cfirst - mixed) / denom
        + second * (csecond - mixed) / denom
        + balance_weight * load
    )
    inner = jnp.sum(probs * upward, axis=1, keepdims=True)
    grad = probs * (upward - inner) + 2.0 * zloss_weight * lse * probs
    return gfirst, gsecond, grad.astype(jnp.bfloat16)


def flip(index, mask, size):
    out = index
    bit = 1
    while bit < size:
        if mask & bit:
            out = out + bit * (1 - 2 * ((index // bit) % 2))
        bit *= 2
    return out


def exchange(
    n, d, capacity, owned,
    tok_hbm, w_hbm, cot_hbm, pick_hbm, slot_hbm,
    gates_ref, wgrad_ref, slots_ref,
    tok_ref, w_ref, cot_ref, pick_ref, slot_ref, aux_rows, aux,
    lg_send, lg_recv, cnt_send, cnt_recv, own_grad, grads, rows_send, part_own, part_send, part_recv, own_wgrad, wgrads,
    in_sems, out_sems, cnt_ss, cnt_rs, lg_ss, lg_rs, gr_ss, gr_rs, a2a_ss, a2a_rs, rs_ss, rs_rs, ag_ss, ag_rs,
):
    me = lax.axis_index("mp")
    my_dp = lax.axis_index("dp")
    rows, feats = tok_ref.shape
    experts = w_ref.shape[0]
    own = rows // n
    half = own // 2
    width = owned * capacity
    eper = experts // d
    f32, bf16 = jnp.float32, jnp.bfloat16
    mp_order = list(range(n - 1, 0, -1))
    dp_order = list(range(d - 1, 0, -1))
    early = [k for k in (1, 2, 4, 0) if k < n]
    middle = [k for k in mp_order if k not in early][:2]
    rest = [k for k in mp_order if k not in early + middle]
    late = [rest[i : i + 4] for i in range(0, len(rest), 4)]
    halves = part_send.shape[0]
    wide = feats // halves
    cuts = tok_ref.shape[0] // 2

    def to_mp(k):
        return {"dp": my_dp, "mp": flip(me, k, n)}

    def to_dp(k):
        return {"dp": flip(my_dp, k, d), "mp": me}

    w_in = pltpu.make_async_copy(w_hbm, w_ref, in_sems.at[1])
    w_in.start()
    tok_in = [
        pltpu.make_async_copy(
            tok_hbm.at[i * cuts : (i + 1) * cuts], tok_ref.at[i * cuts : (i + 1) * cuts],
            in_sems.at[5 * i])
        for i in range(2)
    ]
    for copy in tok_in:
        copy.start()
    small_in = [
        pltpu.make_async_copy(src, dst, in_sems.at[2 + i])
        for i, (src, dst) in enumerate(
            ((pick_hbm, pick_ref), (cot_hbm, cot_ref), (slot_hbm, slot_ref)))
    ]
    for copy in small_in:
        copy.start()
    barrier = pltpu.get_barrier_semaphore()
    for k in mp_order:
        pl.semaphore_signal(barrier, inc=1, device_id=to_mp(k), device_id_type=MESH)
    for k in dp_order:
        pl.semaphore_signal(barrier, inc=1, device_id=to_dp(k), device_id_type=MESH)

    for copy in small_in:
        copy.wait()
    picks = pick_ref[...]
    aux_rows[...] = jnp.zeros_like(aux_rows)
    aux_rows[0:2] = picks.astype(f32)
    aux_rows[2:4] = cot_ref[...]
    aux[...] = jnp.transpose(aux_rows[...])
    levels = lax.broadcasted_iota(jnp.int32, (experts, rows), 0)
    hot = (picks[0:1] == levels).astype(f32) + (picks[1:2] == levels).astype(f32)
    local = lax.dot_general(
        jnp.ones((8, rows), bf16), hot.astype(bf16), (((1,), (1,)), ((), ())), preferred_element_type=f32)
    cnt_send[...] = jnp.concatenate([local, local], axis=1)
    slots = slot_ref[...]
    owner_of = lax.div(picks, jnp.int32(owned))
    cell = jnp.where(slots >= 0, owner_of * width + slots * owned + picks - owner_of * owned, -1)
    place = lax.broadcasted_iota(jnp.int32, (width, rows), 0)

    w_in.wait()
    for i, copy in enumerate(tok_in):
        copy.wait()
        partial_value = lax.dot_general(
            tok_ref[i * cuts : (i + 1) * cuts], w_ref[...], (((1,), (1,)), ((), ())),
            preferred_element_type=f32)
        for p in range(n // 2):
            lo = partial_value[p * own : p * own + half]
            hi = partial_value[p * own + half : (p + 1) * own]
            lg_send[i * (n // 2) + p] = jnp.concatenate([lo, hi], axis=1)

    pl.semaphore_wait(barrier, n - 1 + d - 1)

    lg = {}
    for k in mp_order:
        lg[k] = pltpu.make_async_remote_copy(
            src_ref=lg_send.at[flip(me, k, n)], dst_ref=lg_recv.at[k],
            send_sem=lg_ss.at[k], recv_sem=lg_rs.at[k], device_id=to_mp(k), device_id_type=MESH)
        lg[k].start()
    cnt = {}
    for k in dp_order:
        cnt[k] = pltpu.make_async_remote_copy(
            src_ref=cnt_send, dst_ref=cnt_recv.at[k],
            send_sem=cnt_ss.at[k], recv_sem=cnt_rs.at[k], device_id=to_dp(k), device_id_type=MESH)
        cnt[k].start()

    def fill(batch):
        onehots = []
        for k in batch:
            target = place + flip(me, k, n) * width
            onehots.append(((cell[0:1] == target) | (cell[1:2] == target)).astype(f32))
        onehot = jnp.concatenate(onehots, axis=0).astype(bf16)
        placed = jnp.dot(onehot, tok_ref[...], preferred_element_type=f32).astype(bf16)
        for i, k in enumerate(batch):
            rows_send[k] = placed[i * width : (i + 1) * width]

    columns = pl.ds(pl.multiple_of(me * feats, feats), feats)
    a2a = {}

    def push(k):
        a2a[k] = pltpu.make_async_remote_copy(
            src_ref=rows_send.at[k], dst_ref=slots_ref.at[:, columns],
            send_sem=a2a_ss.at[k], recv_sem=a2a_rs.at[k], device_id=to_mp(k), device_id_type=MESH)
        a2a[k].start()

    fill(early)
    for k in early:
        if k:
            push(k)
    kept = pltpu.make_async_copy(rows_send.at[0], slots_ref.at[:, columns], out_sems.at[0])
    kept.start()

    for k in dp_order:
        cnt[k].wait()
    counts = cnt_send[...]
    for k in dp_order:
        counts = counts + cnt_recv[k]
    load = counts[0:1, :experts] * experts / (2.0 * rows * d)
    for k in mp_order:
        lg[k].wait()
    packed = lg_send[me]
    for k in mp_order:
        packed = packed + lg_recv[k]
    logits = jnp.concatenate([packed[:, :experts], packed[:, experts:]], axis=0)
    mine = pl.ds(pl.multiple_of(me * own, own), own)
    side = aux[mine, :]
    gfirst, gsecond, grad = route_grad(logits, side[:, 2:4], side[:, 0:2], load)
    own_grad[...] = grad
    grads[mine, :] = grad
    gr = {}
    for k in mp_order:
        gr[k] = pltpu.make_async_remote_copy(
            src_ref=own_grad, dst_ref=grads.at[mine, :],
            send_sem=gr_ss.at[k], recv_sem=gr_rs.at[k], device_id=to_mp(k), device_id_type=MESH)
        gr[k].start()
    for batch in [middle] + late:
        if batch:
            fill(batch)
    gates_ref[0:1] = jnp.transpose(jnp.broadcast_to(gfirst, (own, 128)))[0:1]
    gates_ref[1:2] = jnp.transpose(jnp.broadcast_to(gsecond, (own, 128)))[0:1]
    for k in mp_order:
        gr[k].wait()
    for k in middle:
        push(k)

    rs, ag = {}, {}
    for h in range(halves):
        part = lax.dot_general(
            grads[...], tok_ref[:, h * wide : (h + 1) * wide], (((0,), (0,)), ((), ())),
            preferred_element_type=f32)
        for j in range(d):
            part_own[h, j] = part[j * eper : (j + 1) * eper]
            part_send[h, j] = part[j * eper : (j + 1) * eper].astype(bf16)
        for k in dp_order:
            rs[h, k] = pltpu.make_async_remote_copy(
                src_ref=part_send.at[h, flip(my_dp, k, d)], dst_ref=part_recv.at[h, k],
                send_sem=rs_ss.at[h, k], recv_sem=rs_rs.at[h, k],
                device_id=to_dp(k), device_id_type=MESH)
            rs[h, k].start()
    for batch in late:
        for k in batch:
            push(k)
    for h in range(halves):
        for k in dp_order:
            rs[h, k].wait()
        total = part_own[h, my_dp]
        for k in dp_order:
            total = total + part_recv[h, k].astype(f32)
        total = total.astype(bf16)
        own_wgrad[h] = total
        wgrads[h, my_dp] = total
        for k in dp_order:
            ag[h, k] = pltpu.make_async_remote_copy(
                src_ref=own_wgrad.at[h], dst_ref=wgrads.at[h, my_dp],
                send_sem=ag_ss.at[h, k], recv_sem=ag_rs.at[h, k],
                device_id=to_dp(k), device_id_type=MESH)
            ag[h, k].start()
    for h in range(halves):
        for k in dp_order:
            ag[h, k].wait()
        for j in range(d):
            wgrad_ref[j * eper : (j + 1) * eper, h * wide : (h + 1) * wide] = wgrads[h, j].astype(f32)
    for k in mp_order:
        a2a[k].wait()
    kept.wait()


def hand_out(pieces, gates_ref, wgrad_ref, slots_ref, gates_out, wgrad_out, slots_out, sems):
    size = slots_ref.shape[0] // pieces
    chunks = [pl.ds(i * size, size) for i in range(pieces)]
    routes = [(slots_ref.at[c], slots_out.at[c]) for c in chunks]
    routes += [(wgrad_ref, wgrad_out), (gates_ref, gates_out)]
    copies = [pltpu.make_async_copy(a, b, sems.at[i]) for i, (a, b) in enumerate(routes)]
    for copy in copies:
        copy.start()
    for copy in copies:
        copy.wait()


def on_device(n, d, tokens, router_weight, gate_cotangent, expert_index, slot_index):
    rows, feats = tokens.shape
    experts = router_weight.shape[1]
    own = rows // n
    capacity = 5 * rows // (2 * experts)
    owned = experts // n
    width = owned * capacity
    eper = experts // d
    halves = 2
    bf16, f32 = jnp.bfloat16, jnp.float32
    dma = pltpu.SemaphoreType.DMA
    vmem = pl.BlockSpec(memory_space=pltpu.VMEM)
    hbm = pl.BlockSpec(memory_space=pltpu.HBM)
    results = (
        jax.ShapeDtypeStruct((2, own), f32),
        jax.ShapeDtypeStruct((experts, feats), f32),
        jax.ShapeDtypeStruct((width, n * feats), bf16),
    )
    gates, wgrad, slotted = pl.pallas_call(
        functools.partial(exchange, n, d, capacity, owned),
        out_shape=results,
        in_specs=[hbm] * 5,
        out_specs=(vmem,) * 3,
        scratch_shapes=[
            pltpu.VMEM((rows, feats), bf16),
            pltpu.VMEM((experts, feats), bf16),
            pltpu.VMEM((2, rows), f32),
            pltpu.VMEM((2, rows), jnp.int32),
            pltpu.VMEM((2, rows), jnp.int32),
            pltpu.VMEM((8, rows), f32),
            pltpu.VMEM((rows, 8), f32),
            pltpu.VMEM((n, own // 2, 2 * experts), f32),
            pltpu.VMEM((n, own // 2, 2 * experts), f32),
            pltpu.VMEM((8, 2 * experts), f32),
            pltpu.VMEM((d, 8, 2 * experts), f32),
            pltpu.VMEM((own, experts), bf16),
            pltpu.VMEM((rows, experts), bf16),
            pltpu.VMEM((n, width, feats), bf16),
            pltpu.VMEM((halves, d, eper, feats // halves), f32),
            pltpu.VMEM((halves, d, eper, feats // halves), bf16),
            pltpu.VMEM((halves, d, eper, feats // halves), bf16),
            pltpu.VMEM((halves, eper, feats // halves), bf16),
            pltpu.VMEM((halves, d, eper, feats // halves), bf16),
            dma((6,)), dma((1,)),
            dma((d,)), dma((d,)), dma((n,)), dma((n,)), dma((n,)), dma((n,)),
            dma((n,)), dma((n,)), dma((halves, d)), dma((halves, d)), dma((halves, d)), dma((halves, d)),
        ],
        compiler_params=pltpu.CompilerParams(
            collective_id=0, has_side_effects=True, vmem_limit_bytes=24 * 1024 * 1024
        ),
        name="exchange",
    )(*[
        pltpu.with_memory_space_constraint(x, pltpu.HBM)
        for x in (tokens, router_weight.T, gate_cotangent.T, expert_index.T, slot_index.T)
    ])
    pieces = width // 16
    gates, wgrad, slotted = pl.pallas_call(
        functools.partial(hand_out, pieces),
        out_shape=results,
        in_specs=[vmem] * 3,
        out_specs=(hbm,) * 3,
        scratch_shapes=[dma((pieces + 2,))],
        compiler_params=pltpu.CompilerParams(vmem_limit_bytes=16 * 1024 * 1024),
        name="hand_out",
    )(gates, wgrad, slotted)
    dispatched = slotted.reshape(1, capacity, owned, n * feats).transpose(0, 2, 1, 3)
    return gates.T, wgrad.T, dispatched


def solution(mesh):
    n, d = mesh.shape["mp"], mesh.shape["dp"]
    in_specs = (P("dp", "mp"), P("mp", None), P("dp", None), P("dp", None), P("dp", None))
    out_specs = (P(("dp", "mp"), None), P("mp", None), P("dp", "mp", None, None))
    return jax.shard_map(
        functools.partial(on_device, n, d),
        mesh=mesh, in_specs=in_specs, out_specs=out_specs, check_vma=False,
    )
```

```python
import functools

import jax
import jax.numpy as jnp
from jax import lax
from jax.experimental import pallas as pl
from jax.experimental.pallas import tpu as pltpu
from jax.sharding import PartitionSpec as P

balance_weight = 0.5
zloss_weight = 0.02
MESH = pl.DeviceIdType.MESH


def route_grad(logits, cotangent, picks, load):
    levels = lax.broadcasted_iota(jnp.int32, logits.shape, 1).astype(jnp.float32)
    expo = jnp.exp(logits)
    total = jnp.sum(expo, axis=1, keepdims=True)
    probs = expo / total
    lse = jnp.log(total)
    first = (picks[:, 0:1] == levels).astype(jnp.float32)
    second = (picks[:, 1:2] == levels).astype(jnp.float32)
    pfirst = jnp.sum(probs * first, axis=1, keepdims=True)
    psecond = jnp.sum(probs * second, axis=1, keepdims=True)
    denom = pfirst + psecond
    gfirst = pfirst / denom
    gsecond = psecond / denom
    cfirst = cotangent[:, 0:1]
    csecond = cotangent[:, 1:2]
    mixed = cfirst * gfirst + csecond * gsecond
    upward = (
        first * (cfirst - mixed) / denom
        + second * (csecond - mixed) / denom
        + balance_weight * load
    )
    inner = jnp.sum(probs * upward, axis=1, keepdims=True)
    grad = probs * (upward - inner) + 2.0 * zloss_weight * lse * probs
    return gfirst, gsecond, grad.astype(jnp.bfloat16)


def flip(index, mask, size):
    out = index
    bit = 1
    while bit < size:
        if mask & bit:
            out = out + bit * (1 - 2 * ((index // bit) % 2))
        bit *= 2
    return out


def exchange(
    n, d, capacity, owned,
    tok_hbm, w_hbm, cot_hbm, pick_hbm, slot_hbm,
    gates_ref, wgrad_ref, slots_ref,
    tok_ref, w_ref, cot_ref, pick_ref, slot_ref, aux_rows, aux,
    lg_send, lg_recv, cnt_send, cnt_recv, own_grad, grads, rows_send, part_send, part_recv, own_wgrad, wgrads,
    in_sems, out_sems, cnt_ss, cnt_rs, lg_ss, lg_rs, gr_ss, gr_rs, a2a_ss, a2a_rs, rs_ss, rs_rs, ag_ss, ag_rs,
):
    me = lax.axis_index("mp")
    my_dp = lax.axis_index("dp")
    rows, feats = tok_ref.shape
    experts = w_ref.shape[0]
    own = rows // n
    half = own // 2
    width = owned * capacity
    eper = experts // d
    f32, bf16 = jnp.float32, jnp.bfloat16
    mp_order = list(range(n - 1, 0, -1))
    dp_order = list(range(d - 1, 0, -1))
    early = [k for k in (1, 2, 4, 0) if k < n]
    middle = [k for k in mp_order if k not in early][:2]
    rest = [k for k in mp_order if k not in early + middle]
    late = [rest[i : i + 4] for i in range(0, len(rest), 4)]
    halves = part_send.shape[0]
    wide = feats // halves
    cuts = tok_ref.shape[0] // 2

    def to_mp(k):
        return {"dp": my_dp, "mp": flip(me, k, n)}

    def to_dp(k):
        return {"dp": flip(my_dp, k, d), "mp": me}

    w_in = pltpu.make_async_copy(w_hbm, w_ref, in_sems.at[1])
    w_in.start()
    tok_in = [
        pltpu.make_async_copy(
            tok_hbm.at[i * cuts : (i + 1) * cuts], tok_ref.at[i * cuts : (i + 1) * cuts],
            in_sems.at[5 * i])
        for i in range(2)
    ]
    for copy in tok_in:
        copy.start()
    small_in = [
        pltpu.make_async_copy(src, dst, in_sems.at[2 + i])
        for i, (src, dst) in enumerate(
            ((pick_hbm, pick_ref), (cot_hbm, cot_ref), (slot_hbm, slot_ref)))
    ]
    for copy in small_in:
        copy.start()
    barrier = pltpu.get_barrier_semaphore()
    for k in mp_order:
        pl.semaphore_signal(barrier, inc=1, device_id=to_mp(k), device_id_type=MESH)
    for k in dp_order:
        pl.semaphore_signal(barrier, inc=1, device_id=to_dp(k), device_id_type=MESH)

    for copy in small_in:
        copy.wait()
    picks = pick_ref[...]
    aux_rows[...] = jnp.zeros_like(aux_rows)
    aux_rows[0:2] = picks.astype(f32)
    aux_rows[2:4] = cot_ref[...]
    aux[...] = jnp.transpose(aux_rows[...])
    levels = lax.broadcasted_iota(jnp.int32, (experts, rows), 0)
    hot = (picks[0:1] == levels).astype(f32) + (picks[1:2] == levels).astype(f32)
    local = lax.dot_general(
        jnp.ones((8, rows), bf16), hot.astype(bf16), (((1,), (1,)), ((), ())), preferred_element_type=f32)
    cnt_send[...] = jnp.concatenate([local, local], axis=1)
    slots = slot_ref[...]
    owner_of = lax.div(picks, jnp.int32(owned))
    cell = jnp.where(slots >= 0, owner_of * width + slots * owned + picks - owner_of * owned, -1)
    place = lax.broadcasted_iota(jnp.int32, (width, rows), 0)

    w_in.wait()
    for i, copy in enumerate(tok_in):
        copy.wait()
        partial_value = lax.dot_general(
            tok_ref[i * cuts : (i + 1) * cuts], w_ref[...], (((1,), (1,)), ((), ())),
            preferred_element_type=f32)
        for p in range(n // 2):
            lo = partial_value[p * own : p * own + half]
            hi = partial_value[p * own + half : (p + 1) * own]
            lg_send[i * (n // 2) + p] = jnp.concatenate([lo, hi], axis=1)

    pl.semaphore_wait(barrier, n - 1 + d - 1)

    lg = {}
    for k in mp_order:
        lg[k] = pltpu.make_async_remote_copy(
            src_ref=lg_send.at[flip(me, k, n)], dst_ref=lg_recv.at[k],
            send_sem=lg_ss.at[k], recv_sem=lg_rs.at[k], device_id=to_mp(k), device_id_type=MESH)
        lg[k].start()
    cnt = {}
    for k in dp_order:
        cnt[k] = pltpu.make_async_remote_copy(
            src_ref=cnt_send, dst_ref=cnt_recv.at[k],
            send_sem=cnt_ss.at[k], recv_sem=cnt_rs.at[k], device_id=to_dp(k), device_id_type=MESH)
        cnt[k].start()

    def fill(batch):
        onehots = []
        for k in batch:
            target = place + flip(me, k, n) * width
            onehots.append(((cell[0:1] == target) | (cell[1:2] == target)).astype(f32))
        onehot = jnp.concatenate(onehots, axis=0).astype(bf16)
        placed = jnp.dot(onehot, tok_ref[...], preferred_element_type=f32).astype(bf16)
        for i, k in enumerate(batch):
            rows_send[k] = placed[i * width : (i + 1) * width]

    columns = pl.ds(pl.multiple_of(me * feats, feats), feats)
    a2a = {}

    def push(k):
        a2a[k] = pltpu.make_async_remote_copy(
            src_ref=rows_send.at[k], dst_ref=slots_ref.at[:, columns],
            send_sem=a2a_ss.at[k], recv_sem=a2a_rs.at[k], device_id=to_mp(k), device_id_type=MESH)
        a2a[k].start()

    fill(early)
    for k in early:
        if k:
            push(k)
    kept = pltpu.make_async_copy(rows_send.at[0], slots_ref.at[:, columns], out_sems.at[0])
    kept.start()

    for k in dp_order:
        cnt[k].wait()
    counts = cnt_send[...]
    for k in dp_order:
        counts = counts + cnt_recv[k]
    load = counts[0:1, :experts] * experts / (2.0 * rows * d)
    for k in mp_order:
        lg[k].wait()
    packed = lg_send[me]
    for k in mp_order:
        packed = packed + lg_recv[k]
    logits = jnp.concatenate([packed[:, :experts], packed[:, experts:]], axis=0)
    mine = pl.ds(pl.multiple_of(me * own, own), own)
    side = aux[mine, :]
    gfirst, gsecond, grad = route_grad(logits, side[:, 2:4], side[:, 0:2], load)
    own_grad[...] = grad
    grads[mine, :] = grad
    gr = {}
    for k in mp_order:
        gr[k] = pltpu.make_async_remote_copy(
            src_ref=own_grad, dst_ref=grads.at[mine, :],
            send_sem=gr_ss.at[k], recv_sem=gr_rs.at[k], device_id=to_mp(k), device_id_type=MESH)
        gr[k].start()
    gates_ref[0:1] = jnp.transpose(jnp.broadcast_to(gfirst, (own, 128)))[0:1]
    gates_ref[1:2] = jnp.transpose(jnp.broadcast_to(gsecond, (own, 128)))[0:1]
    if middle:
        fill(middle)
    for k in middle:
        push(k)
    for batch in late:
        fill(batch)
    for k in mp_order:
        gr[k].wait()

    rs, ag = {}, {}
    for h in range(halves):
        part = lax.dot_general(
            grads[...], tok_ref[:, h * wide : (h + 1) * wide], (((0,), (0,)), ((), ())),
            preferred_element_type=f32)
        for j in range(d):
            part_send[h, j] = part[j * eper : (j + 1) * eper]
        for k in dp_order:
            rs[h, k] = pltpu.make_async_remote_copy(
                src_ref=part_send.at[h, flip(my_dp, k, d)], dst_ref=part_recv.at[h, k],
                send_sem=rs_ss.at[h, k], recv_sem=rs_rs.at[h, k],
                device_id=to_dp(k), device_id_type=MESH)
            rs[h, k].start()
    for batch in late:
        for k in batch:
            push(k)
    for h in range(halves):
        for k in dp_order:
            rs[h, k].wait()
        total = part_send[h, my_dp]
        for k in dp_order:
            total = total + part_recv[h, k]
        total = total.astype(bf16)
        own_wgrad[h] = total
        wgrads[h, my_dp] = total
        for k in dp_order:
            ag[h, k] = pltpu.make_async_remote_copy(
                src_ref=own_wgrad.at[h], dst_ref=wgrads.at[h, my_dp],
                send_sem=ag_ss.at[h, k], recv_sem=ag_rs.at[h, k],
                device_id=to_dp(k), device_id_type=MESH)
            ag[h, k].start()
    for h in range(halves):
        for k in dp_order:
            ag[h, k].wait()
        for j in range(d):
            wgrad_ref[j * eper : (j + 1) * eper, h * wide : (h + 1) * wide] = wgrads[h, j].astype(f32)
    for k in mp_order:
        a2a[k].wait()
    kept.wait()


def hand_out(pieces, gates_ref, wgrad_ref, slots_ref, gates_out, wgrad_out, slots_out, sems):
    size = slots_ref.shape[0] // pieces
    chunks = [pl.ds(i * size, size) for i in range(pieces)]
    routes = [(slots_ref.at[c], slots_out.at[c]) for c in chunks]
    routes += [(wgrad_ref, wgrad_out), (gates_ref, gates_out)]
    copies = [pltpu.make_async_copy(a, b, sems.at[i]) for i, (a, b) in enumerate(routes)]
    for copy in copies:
        copy.start()
    for copy in copies:
        copy.wait()


def on_device(n, d, tokens, router_weight, gate_cotangent, expert_index, slot_index):
    rows, feats = tokens.shape
    experts = router_weight.shape[1]
    own = rows // n
    capacity = 5 * rows // (2 * experts)
    owned = experts // n
    width = owned * capacity
    eper = experts // d
    halves = 2
    bf16, f32 = jnp.bfloat16, jnp.float32
    dma = pltpu.SemaphoreType.DMA
    vmem = pl.BlockSpec(memory_space=pltpu.VMEM)
    hbm = pl.BlockSpec(memory_space=pltpu.HBM)
    results = (
        jax.ShapeDtypeStruct((2, own), f32),
        jax.ShapeDtypeStruct((experts, feats), f32),
        jax.ShapeDtypeStruct((width, n * feats), bf16),
    )
    gates, wgrad, slotted = pl.pallas_call(
        functools.partial(exchange, n, d, capacity, owned),
        out_shape=results,
        in_specs=[hbm] * 5,
        out_specs=(vmem,) * 3,
        scratch_shapes=[
            pltpu.VMEM((rows, feats), bf16),
            pltpu.VMEM((experts, feats), bf16),
            pltpu.VMEM((2, rows), f32),
            pltpu.VMEM((2, rows), jnp.int32),
            pltpu.VMEM((2, rows), jnp.int32),
            pltpu.VMEM((8, rows), f32),
            pltpu.VMEM((rows, 8), f32),
            pltpu.VMEM((n, own // 2, 2 * experts), f32),
            pltpu.VMEM((n, own // 2, 2 * experts), f32),
            pltpu.VMEM((8, 2 * experts), f32),
            pltpu.VMEM((d, 8, 2 * experts), f32),
            pltpu.VMEM((own, experts), bf16),
            pltpu.VMEM((rows, experts), bf16),
            pltpu.VMEM((n, width, feats), bf16),
            pltpu.VMEM((halves, d, eper, feats // halves), f32),
            pltpu.VMEM((halves, d, eper, feats // halves), f32),
            pltpu.VMEM((halves, eper, feats // halves), bf16),
            pltpu.VMEM((halves, d, eper, feats // halves), bf16),
            dma((6,)), dma((1,)),
            dma((d,)), dma((d,)), dma((n,)), dma((n,)), dma((n,)), dma((n,)),
            dma((n,)), dma((n,)), dma((halves, d)), dma((halves, d)), dma((halves, d)), dma((halves, d)),
        ],
        compiler_params=pltpu.CompilerParams(
            collective_id=0, has_side_effects=True, vmem_limit_bytes=24 * 1024 * 1024
        ),
        name="exchange",
    )(*[
        pltpu.with_memory_space_constraint(x, pltpu.HBM)
        for x in (tokens, router_weight.T, gate_cotangent.T, expert_index.T, slot_index.T)
    ])
    pieces = width // 16
    gates, wgrad, slotted = pl.pallas_call(
        functools.partial(hand_out, pieces),
        out_shape=results,
        in_specs=[vmem] * 3,
        out_specs=(hbm,) * 3,
        scratch_shapes=[dma((pieces + 2,))],
        compiler_params=pltpu.CompilerParams(vmem_limit_bytes=16 * 1024 * 1024),
        name="hand_out",
    )(gates, wgrad, slotted)
    dispatched = slotted.reshape(1, capacity, owned, n * feats).transpose(0, 2, 1, 3)
    return gates.T, wgrad.T, dispatched


def solution(mesh):
    n, d = mesh.shape["mp"], mesh.shape["dp"]
    in_specs = (P("dp", "mp"), P("mp", None), P("dp", None), P("dp", None), P("dp", None))
    out_specs = (P(("dp", "mp"), None), P("mp", None), P("dp", "mp", None, None))
    return jax.shard_map(
        functools.partial(on_device, n, d),
        mesh=mesh, in_specs=in_specs, out_specs=out_specs, check_vma=False,
    )
```

```python
import functools

import jax
import jax.numpy as jnp
from jax import lax
from jax.experimental import pallas as pl
from jax.experimental.pallas import tpu as pltpu
from jax.sharding import PartitionSpec as P

balance_weight = 0.5
zloss_weight = 0.02
MESH = pl.DeviceIdType.MESH


def route_grad(logits, cotangent, picks, load):
    levels = lax.broadcasted_iota(jnp.int32, logits.shape, 1).astype(jnp.float32)
    expo = jnp.exp(logits)
    total = jnp.sum(expo, axis=1, keepdims=True)
    probs = expo / total
    lse = jnp.log(total)
    first = (picks[:, 0:1] == levels).astype(jnp.float32)
    second = (picks[:, 1:2] == levels).astype(jnp.float32)
    pfirst = jnp.sum(probs * first, axis=1, keepdims=True)
    psecond = jnp.sum(probs * second, axis=1, keepdims=True)
    denom = pfirst + psecond
    gfirst = pfirst / denom
    gsecond = psecond / denom
    cfirst = cotangent[:, 0:1]
    csecond = cotangent[:, 1:2]
    mixed = cfirst * gfirst + csecond * gsecond
    upward = (
        first * (cfirst - mixed) / denom
        + second * (csecond - mixed) / denom
        + balance_weight * load
    )
    inner = jnp.sum(probs * upward, axis=1, keepdims=True)
    grad = probs * (upward - inner) + 2.0 * zloss_weight * lse * probs
    return gfirst, gsecond, grad.astype(jnp.bfloat16)


def flip(index, mask, size):
    out = index
    bit = 1
    while bit < size:
        if mask & bit:
            out = out + bit * (1 - 2 * ((index // bit) % 2))
        bit *= 2
    return out


def exchange(
    n, d, capacity, owned,
    tok_hbm, w_hbm, cot_hbm, pick_hbm, slot_hbm,
    gates_ref, wgrad_ref, slots_ref,
    tok_ref, w_ref, cot_ref, pick_ref, slot_ref, aux_rows, aux,
    lg_send, lg_recv, cnt_send, cnt_recv, own_grad, grads, rows_send, part_send, part_recv, own_wgrad, wgrads,
    in_sems, out_sems, cnt_ss, cnt_rs, lg_ss, lg_rs, gr_ss, gr_rs, a2a_ss, a2a_rs, rs_ss, rs_rs, ag_ss, ag_rs,
):
    me = lax.axis_index("mp")
    my_dp = lax.axis_index("dp")
    rows, feats = tok_ref.shape
    experts = w_ref.shape[0]
    own = rows // n
    half = own // 2
    width = owned * capacity
    eper = experts // d
    f32, bf16 = jnp.float32, jnp.bfloat16
    mp_order = list(range(n - 1, 0, -1))
    dp_order = list(range(d - 1, 0, -1))
    early = [k for k in (1, 2, 4, 0) if k < n]
    middle = [k for k in mp_order if k not in early][:3]
    rest = [k for k in mp_order if k not in early + middle]
    late = [rest[i : i + 4] for i in range(0, len(rest), 4)]
    halves = part_send.shape[0]
    wide = feats // halves
    cuts = tok_ref.shape[0] // 2

    def to_mp(k):
        return {"dp": my_dp, "mp": flip(me, k, n)}

    def to_dp(k):
        return {"dp": flip(my_dp, k, d), "mp": me}

    w_in = pltpu.make_async_copy(w_hbm, w_ref, in_sems.at[1])
    w_in.start()
    tok_in = [
        pltpu.make_async_copy(
            tok_hbm.at[i * cuts : (i + 1) * cuts], tok_ref.at[i * cuts : (i + 1) * cuts],
            in_sems.at[5 * i])
        for i in range(2)
    ]
    for copy in tok_in:
        copy.start()
    small_in = [
        pltpu.make_async_copy(src, dst, in_sems.at[2 + i])
        for i, (src, dst) in enumerate(
            ((pick_hbm, pick_ref), (cot_hbm, cot_ref), (slot_hbm, slot_ref)))
    ]
    for copy in small_in:
        copy.start()
    barrier = pltpu.get_barrier_semaphore()
    for k in mp_order:
        pl.semaphore_signal(barrier, inc=1, device_id=to_mp(k), device_id_type=MESH)
    for k in dp_order:
        pl.semaphore_signal(barrier, inc=1, device_id=to_dp(k), device_id_type=MESH)

    for copy in small_in:
        copy.wait()
    picks = pick_ref[...]
    aux_rows[...] = jnp.zeros_like(aux_rows)
    aux_rows[0:2] = picks.astype(f32)
    aux_rows[2:4] = cot_ref[...]
    aux[...] = jnp.transpose(aux_rows[...])
    levels = lax.broadcasted_iota(jnp.int32, (experts, rows), 0)
    hot = (picks[0:1] == levels).astype(f32) + (picks[1:2] == levels).astype(f32)
    local = lax.dot_general(
        jnp.ones((8, rows), bf16), hot.astype(bf16), (((1,), (1,)), ((), ())), preferred_element_type=f32)
    cnt_send[...] = jnp.concatenate([local, local], axis=1)
    slots = slot_ref[...]
    owner_of = lax.div(picks, jnp.int32(owned))
    cell = jnp.where(slots >= 0, owner_of * width + slots * owned + picks - owner_of * owned, -1)
    place = lax.broadcasted_iota(jnp.int32, (width, rows), 0)

    w_in.wait()
    for i, copy in enumerate(tok_in):
        copy.wait()
        partial_value = lax.dot_general(
            tok_ref[i * cuts : (i + 1) * cuts], w_ref[...], (((1,), (1,)), ((), ())),
            preferred_element_type=f32)
        for p in range(n // 2):
            lo = partial_value[p * own : p * own + half]
            hi = partial_value[p * own + half : (p + 1) * own]
            lg_send[i * (n // 2) + p] = jnp.concatenate([lo, hi], axis=1)

    pl.semaphore_wait(barrier, n - 1 + d - 1)

    lg = {}
    for k in mp_order:
        lg[k] = pltpu.make_async_remote_copy(
            src_ref=lg_send.at[flip(me, k, n)], dst_ref=lg_recv.at[k],
            send_sem=lg_ss.at[k], recv_sem=lg_rs.at[k], device_id=to_mp(k), device_id_type=MESH)
        lg[k].start()
    cnt = {}
    for k in dp_order:
        cnt[k] = pltpu.make_async_remote_copy(
            src_ref=cnt_send, dst_ref=cnt_recv.at[k],
            send_sem=cnt_ss.at[k], recv_sem=cnt_rs.at[k], device_id=to_dp(k), device_id_type=MESH)
        cnt[k].start()

    def fill(batch):
        onehots = []
        for k in batch:
            target = place + flip(me, k, n) * width
            onehots.append(((cell[0:1] == target) | (cell[1:2] == target)).astype(f32))
        onehot = jnp.concatenate(onehots, axis=0).astype(bf16)
        placed = jnp.dot(onehot, tok_ref[...], preferred_element_type=f32).astype(bf16)
        for i, k in enumerate(batch):
            rows_send[k] = placed[i * width : (i + 1) * width]

    columns = pl.ds(pl.multiple_of(me * feats, feats), feats)
    a2a = {}

    def push(k):
        a2a[k] = pltpu.make_async_remote_copy(
            src_ref=rows_send.at[k], dst_ref=slots_ref.at[:, columns],
            send_sem=a2a_ss.at[k], recv_sem=a2a_rs.at[k], device_id=to_mp(k), device_id_type=MESH)
        a2a[k].start()

    fill(early)
    for k in early:
        if k:
            push(k)
    kept = pltpu.make_async_copy(rows_send.at[0], slots_ref.at[:, columns], out_sems.at[0])
    kept.start()

    for k in dp_order:
        cnt[k].wait()
    counts = cnt_send[...]
    for k in dp_order:
        counts = counts + cnt_recv[k]
    load = counts[0:1, :experts] * experts / (2.0 * rows * d)
    for k in mp_order:
        lg[k].wait()
    packed = lg_send[me]
    for k in mp_order:
        packed = packed + lg_recv[k]
    logits = jnp.concatenate([packed[:, :experts], packed[:, experts:]], axis=0)
    mine = pl.ds(pl.multiple_of(me * own, own), own)
    side = aux[mine, :]
    gfirst, gsecond, grad = route_grad(logits, side[:, 2:4], side[:, 0:2], load)
    own_grad[...] = grad
    grads[mine, :] = grad
    gr = {}
    for k in mp_order:
        gr[k] = pltpu.make_async_remote_copy(
            src_ref=own_grad, dst_ref=grads.at[mine, :],
            send_sem=gr_ss.at[k], recv_sem=gr_rs.at[k], device_id=to_mp(k), device_id_type=MESH)
        gr[k].start()
    gates_ref[0:1] = jnp.transpose(jnp.broadcast_to(gfirst, (own, 128)))[0:1]
    gates_ref[1:2] = jnp.transpose(jnp.broadcast_to(gsecond, (own, 128)))[0:1]
    if middle:
        fill(middle)
    for k in middle:
        push(k)
    for batch in late:
        fill(batch)
    for k in mp_order:
        gr[k].wait()

    rs, ag = {}, {}
    for h in range(halves):
        part = lax.dot_general(
            grads[...], tok_ref[:, h * wide : (h + 1) * wide], (((0,), (0,)), ((), ())),
            preferred_element_type=f32)
        for j in range(d):
            part_send[h, j] = part[j * eper : (j + 1) * eper]
        for k in dp_order:
            rs[h, k] = pltpu.make_async_remote_copy(
                src_ref=part_send.at[h, flip(my_dp, k, d)], dst_ref=part_recv.at[h, k],
                send_sem=rs_ss.at[h, k], recv_sem=rs_rs.at[h, k],
                device_id=to_dp(k), device_id_type=MESH)
            rs[h, k].start()
    for batch in late:
        for k in batch:
            push(k)
    for h in range(halves):
        for k in dp_order:
            rs[h, k].wait()
        total = part_send[h, my_dp]
        for k in dp_order:
            total = total + part_recv[h, k]
        total = total.astype(bf16)
        own_wgrad[h] = total
        wgrads[h, my_dp] = total
        for k in dp_order:
            ag[h, k] = pltpu.make_async_remote_copy(
                src_ref=own_wgrad.at[h], dst_ref=wgrads.at[h, my_dp],
                send_sem=ag_ss.at[h, k], recv_sem=ag_rs.at[h, k],
                device_id=to_dp(k), device_id_type=MESH)
            ag[h, k].start()
    for h in range(halves):
        for k in dp_order:
            ag[h, k].wait()
        for j in range(d):
            wgrad_ref[j * eper : (j + 1) * eper, h * wide : (h + 1) * wide] = wgrads[h, j].astype(f32)
    for k in mp_order:
        a2a[k].wait()
    kept.wait()


def hand_out(pieces, gates_ref, wgrad_ref, slots_ref, gates_out, wgrad_out, slots_out, sems):
    size = slots_ref.shape[0] // pieces
    chunks = [pl.ds(i * size, size) for i in range(pieces)]
    routes = [(slots_ref.at[c], slots_out.at[c]) for c in chunks]
    routes += [(wgrad_ref, wgrad_out), (gates_ref, gates_out)]
    copies = [pltpu.make_async_copy(a, b, sems.at[i]) for i, (a, b) in enumerate(routes)]
    for copy in copies:
        copy.start()
    for copy in copies:
        copy.wait()


def on_device(n, d, tokens, router_weight, gate_cotangent, expert_index, slot_index):
    rows, feats = tokens.shape
    experts = router_weight.shape[1]
    own = rows // n
    capacity = 5 * rows // (2 * experts)
    owned = experts // n
    width = owned * capacity
    eper = experts // d
    halves = 2
    bf16, f32 = jnp.bfloat16, jnp.float32
    dma = pltpu.SemaphoreType.DMA
    vmem = pl.BlockSpec(memory_space=pltpu.VMEM)
    hbm = pl.BlockSpec(memory_space=pltpu.HBM)
    results = (
        jax.ShapeDtypeStruct((2, own), f32),
        jax.ShapeDtypeStruct((experts, feats), f32),
        jax.ShapeDtypeStruct((width, n * feats), bf16),
    )
    gates, wgrad, slotted = pl.pallas_call(
        functools.partial(exchange, n, d, capacity, owned),
        out_shape=results,
        in_specs=[hbm] * 5,
        out_specs=(vmem,) * 3,
        scratch_shapes=[
            pltpu.VMEM((rows, feats), bf16),
            pltpu.VMEM((experts, feats), bf16),
            pltpu.VMEM((2, rows), f32),
            pltpu.VMEM((2, rows), jnp.int32),
            pltpu.VMEM((2, rows), jnp.int32),
            pltpu.VMEM((8, rows), f32),
            pltpu.VMEM((rows, 8), f32),
            pltpu.VMEM((n, own // 2, 2 * experts), f32),
            pltpu.VMEM((n, own // 2, 2 * experts), f32),
            pltpu.VMEM((8, 2 * experts), f32),
            pltpu.VMEM((d, 8, 2 * experts), f32),
            pltpu.VMEM((own, experts), bf16),
            pltpu.VMEM((rows, experts), bf16),
            pltpu.VMEM((n, width, feats), bf16),
            pltpu.VMEM((halves, d, eper, feats // halves), f32),
            pltpu.VMEM((halves, d, eper, feats // halves), f32),
            pltpu.VMEM((halves, eper, feats // halves), bf16),
            pltpu.VMEM((halves, d, eper, feats // halves), bf16),
            dma((6,)), dma((1,)),
            dma((d,)), dma((d,)), dma((n,)), dma((n,)), dma((n,)), dma((n,)),
            dma((n,)), dma((n,)), dma((halves, d)), dma((halves, d)), dma((halves, d)), dma((halves, d)),
        ],
        compiler_params=pltpu.CompilerParams(
            collective_id=0, has_side_effects=True, vmem_limit_bytes=24 * 1024 * 1024
        ),
        name="exchange",
    )(*[
        pltpu.with_memory_space_constraint(x, pltpu.HBM)
        for x in (tokens, router_weight.T, gate_cotangent.T, expert_index.T, slot_index.T)
    ])
    pieces = width // 16
    gates, wgrad, slotted = pl.pallas_call(
        functools.partial(hand_out, pieces),
        out_shape=results,
        in_specs=[vmem] * 3,
        out_specs=(hbm,) * 3,
        scratch_shapes=[dma((pieces + 2,))],
        compiler_params=pltpu.CompilerParams(vmem_limit_bytes=16 * 1024 * 1024),
        name="hand_out",
    )(gates, wgrad, slotted)
    dispatched = slotted.reshape(1, capacity, owned, n * feats).transpose(0, 2, 1, 3)
    return gates.T, wgrad.T, dispatched


def solution(mesh):
    n, d = mesh.shape["mp"], mesh.shape["dp"]
    in_specs = (P("dp", "mp"), P("mp", None), P("dp", None), P("dp", None), P("dp", None))
    out_specs = (P(("dp", "mp"), None), P("mp", None), P("dp", "mp", None, None))
    return jax.shard_map(
        functools.partial(on_device, n, d),
        mesh=mesh, in_specs=in_specs, out_specs=out_specs, check_vma=False,
    )
```
